32 devices in a mesh: batch: 16 (over z, y, core), tensor: 2 (over x).
Axes of the slice: x: 2, y: 2, z: 4, core: 2. Of those that a mesh axis runs over, the one named last changes fastest.
Arguments:
- activations: bfloat16 [65536, 768], P(('batch', 'tensor')), may hold values from -6 to 6
- cotangent: float32 [65536, 768], P(('batch', 'tensor')), may hold values from -6 to 6
- buckets: int32 [16], replicated, may hold values from 0 to 2, as said below
- lengths: int32 [16, 4], P('batch'), may hold values from 0 to 4096, as said below
- first_gain: bfloat16 [768], P(('batch', 'tensor')), may hold values from 0.5 to 1.5
- first_bias: bfloat16 [768], P(('batch', 'tensor')), may hold values from -2.5 to 2.5
- in_weight: bfloat16 [768, 2304], P(('batch', 'tensor')), may hold values from -0.21875 to 0.21875
- in_bias: bfloat16 [2304], P(('batch', 'tensor')), may hold values from -2.5 to 2.5
- short_kernel: bfloat16 [3, 768], P(None, ('batch', 'tensor')), may hold values from -3 to 3
- short_value: bfloat16 [3, 768], P(None, ('batch', 'tensor')), may hold values from -3 to 3
- out_weight: bfloat16 [768, 768], P(('batch', 'tensor')), may hold values from -0.3125 to 0.3125
- out_bias: bfloat16 [768], P(('batch', 'tensor')), may hold values from -2.5 to 2.5
- second_gain: bfloat16 [768], P(('batch', 'tensor')), may hold values from 0.5 to 1.5
- second_bias: bfloat16 [768], P(('batch', 'tensor')), may hold values from -2.5 to 2.5
- gate_weight: bfloat16 [768, 3072], P('batch', 'tensor'), may hold values from -0.21875 to 0.21875
- up_weight: bfloat16 [768, 3072], P('batch', 'tensor'), may hold values from -0.21875 to 0.21875
- down_weight: bfloat16 [3072, 768], P('tensor', 'batch'), may hold values from -0.15625 to 0.15625
Outputs:
- out_rows: float32 [65536, 768], P(('batch', 'tensor'))
- grad_activations: float32 [65536, 768], P(('batch', 'tensor'))
- grad_first_gain: float32 [768], P(('batch', 'tensor'))
- grad_first_bias: float32 [768], P(('batch', 'tensor'))
- grad_in_weight: float32 [768, 2304], P(('batch', 'tensor'))
- grad_in_bias: float32 [2304], P(('batch', 'tensor'))
- grad_short_kernel: float32 [3, 768], P(None, ('batch', 'tensor'))
- grad_short_value: float32 [3, 768], P(None, ('batch', 'tensor'))
- grad_out_weight: float32 [768, 768], P(('batch', 'tensor'))
- grad_out_bias: float32 [768], P(('batch', 'tensor'))
- grad_second_gain: float32 [768], P(('batch', 'tensor'))
- grad_second_bias: float32 [768], P(('batch', 'tensor'))
- grad_gate_weight: float32 [768, 3072], P('batch', 'tensor')
- grad_up_weight: float32 [768, 3072], P('batch', 'tensor')
- grad_down_weight: float32 [3072, 768], P('tensor', 'batch')
- norms: float32 [768], P(('batch', 'tensor'))
The draws below stay inside these ranges and needn't reach their ends.
Inputs may be any that keep to these rules, and one draw needn't show every extreme that they name: The slots of batch index b are 4096 >> buckets[b] long. Batch index 0 always has bucket 0. Row b holds the lengths of the 2 ** buckets[b] sequences of batch index b in its first entries and 0 in the rest; each length is more than half of its slot and at most the slot. The first sequence of batch index 0 fills all 4096 slots.
All inputs are finite; a program needn't handle non-finite values.
Results may differ from the reference program's by a relative error of at most 0.015.
Values may be sent and summed in bfloat16 or wider, within the bound.
A program may use at most 1.0625 GiB of HBM per device.

```python
from functools import partial
import jax
import jax.numpy as jnp
from jax import lax

D = 768
FF = 3072
BIN = 4096
TOKENS = 65536
N_BATCH = 16


def bucket_law(key):
    drawn = jax.random.randint(jax.random.fold_in(key, 7), (N_BATCH,), 0, 3, dtype=jnp.int32)
    return drawn.at[0].set(0)


def draw_buckets(key, part):
    shared = bucket_law(key)
    return shared


def draw_lengths(key, part):
    shared = bucket_law(key)
    key = jax.random.fold_in(key, 2)
    slot_width = jnp.right_shift(jnp.int32(BIN), shared)[:, None]
    slot_count = jnp.left_shift(jnp.ones_like(shared), shared)[:, None]
    slot_index = jnp.arange(4, dtype=jnp.int32)[None, :]
    shorter = jax.random.randint(key, (N_BATCH, 4), 0, slot_width // 2, dtype=jnp.int32)
    filled = (slot_width - shorter).at[0, 0].set(BIN)
    return jnp.where(slot_index < slot_count, filled, 0).astype(jnp.int32)


def shard_levels(rng, extent, pieces, least, high):
    factor_of = 1.0
    for axis_at, blocks in pieces:
        heights = jax.random.uniform(jax.random.fold_in(jax.random.fold_in(rng, 6), axis_at), (blocks,), jnp.float32, least / len(pieces), high / len(pieces))
        factor_of = factor_of * jnp.repeat(jnp.exp(heights), extent[axis_at] // blocks).reshape((-1,) + (1,) * (len(extent) - 1 - axis_at))
    return factor_of


def gaussian(key, dims, spread, most, shards=(), kind=jnp.bfloat16):
    array = jax.random.normal(key, dims, jnp.float32) * spread
    if len(shards) > 0:
        array = shard_levels(key, dims, shards, -0.22, 0.18) * array
    return jnp.clip(array, min=-most, max=most).astype(kind)


def setup_inputs(seed: int = 0) -> dict:
    key_of = jax.random.split(jax.random.key(seed), 18)
    return {
        "activations": gaussian(key_of[0], (TOKENS, D), 1.0, 6.0, ((0, 32),)),
        "cotangent": gaussian(key_of[1], (TOKENS, D), 1.0, 6.0, ((0, 32),), jnp.float32),
        "buckets": draw_buckets(jax.random.fold_in(key_of[17], 71), 0),
        "lengths": draw_lengths(jax.random.fold_in(key_of[17], 71), 0),
        "first_gain": jnp.clip(1.0 + 0.1 * jax.random.normal(key_of[4], (D,), jnp.float32), 0.5, 1.5).astype(jnp.bfloat16),
        "first_bias": gaussian(key_of[5], (D,), 0.3, 2.5, ((0, 32),)),
        "in_weight": gaussian(key_of[6], (D, 3 * D), D ** -0.5, 0.21875, ((0, 32),)),
        "in_bias": gaussian(key_of[7], (3 * D,), 0.3, 2.5, ((0, 32),)),
        "short_kernel": gaussian(key_of[8], (3, D), 0.6, 3.0, ((1, 32),)),
        "short_value": gaussian(key_of[9], (3, D), 0.6, 3.0, ((1, 32),)),
        "out_weight": gaussian(key_of[10], (D, D), (D // 2) ** -0.5, 0.3125, ((0, 32),)),
        "out_bias": gaussian(key_of[11], (D,), 0.3, 2.5, ((0, 32),)),
        "second_gain": jnp.clip(1.0 + 0.1 * jax.random.normal(key_of[12], (D,), jnp.float32), 0.5, 1.5).astype(jnp.bfloat16),
        "second_bias": gaussian(key_of[13], (D,), 0.3, 2.5, ((0, 32),)),
        "gate_weight": gaussian(key_of[14], (D, FF), D ** -0.5, 0.21875, ((0, 16), (1, 2))),
        "up_weight": gaussian(key_of[15], (D, FF), D ** -0.5, 0.21875, ((0, 16), (1, 2))),
        "down_weight": gaussian(key_of[16], (FF, D), (FF // 2) ** -0.5, 0.15625, ((0, 2), (1, 16))),
    }


EPS = 1e-05
TINY = 1e-06
HIGH = lax.Precision.HIGHEST

@jax.custom_vjp
def low(v):
    return lax.optimization_barrier(v.astype(jnp.bfloat16)).astype(jnp.float32)

@jax.custom_vjp
def low_back(v):
    return v

def low_keep(v):
    return (low(v), None)

def low_pass(kept, grad):
    return (grad,)

def back_keep(v):
    return (v, None)

def back_low(kept, grad):
    return (low(grad),)
low.defvjp(low_keep, low_pass)
low_back.defvjp(back_keep, back_low)

def layer_norm(values, gain, bias):
    row_mean = lax.optimization_barrier(jnp.mean(values, -1, keepdims=True))
    centred = values - row_mean
    row_var = lax.optimization_barrier(jnp.mean(centred * centred, -1, keepdims=True))
    return centred * lax.rsqrt(row_var + EPS) * gain + bias

def matmul(left, right):
    return jnp.dot(left, right, precision=HIGH, preferred_element_type=jnp.float32)

def short_mix(slots, taps, slot_mask):
    slot_width = slots.shape[1]
    one_back = jnp.pad(slots, ((0, 0), (1, 0), (0, 0)))[:, :slot_width]
    two_back = jnp.pad(slots, ((0, 0), (2, 0), (0, 0)))[:, :slot_width]
    return (taps[0] * slots + taps[1] * one_back + taps[2] * two_back) * slot_mask

def slot_conv(slot_width, kernels, values, short_kernel, short_value, valid_rows):
    slot_count = kernels.shape[0] // slot_width
    channels = kernels.shape[1]
    slot_mask = valid_rows.reshape(slot_count, slot_width, 1)
    kernel_short = short_mix(kernels.reshape(slot_count, slot_width, channels), short_kernel, slot_mask)
    value_short = short_mix(values.reshape(slot_count, slot_width, channels), short_value, slot_mask)
    kernel_norm = jnp.sqrt(lax.optimization_barrier(jnp.sum(kernel_short * kernel_short, 1, keepdims=True)) + TINY)
    kernel_unit = kernel_short / kernel_norm
    unit_spec = jnp.fft.rfft(kernel_unit, n=2 * slot_width, axis=1)
    value_spec = jnp.fft.rfft(value_short, n=2 * slot_width, axis=1)
    power = jnp.real(unit_spec) ** 2 + jnp.imag(unit_spec) ** 2
    conv_out = jnp.fft.irfft(power * value_spec, n=2 * slot_width, axis=1)[:, :slot_width]
    return (conv_out.reshape(kernels.shape).astype(jnp.float32), lax.optimization_barrier(jnp.sum(kernel_norm[:, 0, :], 0)))

def bin_mask(bucket_here, seq_lengths):
    position = jnp.arange(BIN, dtype=jnp.int32)
    slot_width = jnp.right_shift(jnp.int32(BIN), bucket_here.astype(jnp.int32))
    slot_index = position // slot_width
    within = position - slot_index * slot_width
    choose = slot_index[:, None] == jnp.arange(4, dtype=jnp.int32)[None, :]
    slot_limit = lax.optimization_barrier(jnp.sum(jnp.where(choose, seq_lengths[None, :].astype(jnp.int32), 0), 1))
    return (within < slot_limit).astype(jnp.float32)[:, None]

def bin_forward(params, bin_rows, bucket_here, seq_lengths):
    first_gain, first_bias, in_weight, in_bias, short_kernel, short_value, out_weight, out_bias, second_gain, second_bias, gate_weight, up_weight, down_weight = params
    width = bin_rows.shape[1]
    valid_rows = bin_mask(bucket_here, seq_lengths)
    normed_first = low(layer_norm(bin_rows, first_gain, first_bias))
    projected = low_back(matmul(normed_first, in_weight) + in_bias)
    queries = projected[:, :width]
    kernels = low(low_back(projected[:, width:2 * width])) * valid_rows
    values = low(low_back(projected[:, 2 * width:])) * valid_rows
    branches = [partial(slot_conv, BIN >> bucket_level) for bucket_level in range(3)]
    conv_out, norm_sum = lax.switch(bucket_here, branches, kernels, values, short_kernel, short_value, valid_rows)
    mixed = low(low_back(conv_out * valid_rows))
    gated = low(queries * mixed)
    mixer_out = low_back(matmul(gated, out_weight) + out_bias)
    middle = bin_rows + mixer_out
    normed_second = low(layer_norm(middle, second_gain, second_bias))
    gate_pre = low_back(matmul(normed_second, gate_weight))
    up_value = low_back(matmul(normed_second, up_weight))
    hidden = low(jax.nn.silu(gate_pre) * up_value)
    mlp_out = low_back(matmul(hidden, down_weight))
    return (middle + mlp_out, norm_sum)

def reference(activations, cotangent, buckets, lengths, first_gain, first_bias, in_weight, in_bias, short_kernel, short_value, out_weight, out_bias, second_gain, second_bias, gate_weight, up_weight, down_weight):
    params = tuple((param.astype(jnp.float32) for param in (first_gain, first_bias, in_weight, in_bias, short_kernel, short_value, out_weight, out_bias, second_gain, second_bias, gate_weight, up_weight, down_weight)))
    width = activations.shape[1]
    bins = activations.astype(jnp.float32).reshape(N_BATCH, BIN, width)

    def whole_layer(params, bins):

        def bin_step(norm_carry, bin_item):
            bin_rows, bucket_here, seq_lengths = bin_item
            out_bin, norm_sum = jax.checkpoint(bin_forward)(params, bin_rows, bucket_here, seq_lengths)
            return (norm_carry + norm_sum, out_bin)
        norm_total, out_bins = lax.scan(bin_step, jnp.zeros((width,), jnp.float32), (bins, buckets, lengths))
        return (out_bins, norm_total)
    (out_bins, norm_total), pullback = jax.vjp(whole_layer, params, bins)
    param_grads, bin_grads = pullback((cotangent.astype(jnp.float32).reshape(N_BATCH, BIN, width), jnp.zeros_like(norm_total)))
    g_first_gain, g_first_bias, g_in_weight, g_in_bias, g_short_kernel, g_short_value, g_out_weight, g_out_bias, g_second_gain, g_second_bias, g_gate_weight, g_up_weight, g_down_weight = param_grads
    seq_count = jnp.sum(jnp.left_shift(jnp.ones_like(buckets), buckets)).astype(jnp.float32)
    return (out_bins.reshape(-1, width), bin_grads.reshape(-1, width), g_first_gain, g_first_bias, g_in_weight, g_in_bias, g_short_kernel, g_short_value, g_out_weight, g_out_bias, g_second_gain, g_second_bias, g_gate_weight, g_up_weight, g_down_weight, norm_total / seq_count)
```

```python
import math

import jax
import jax.numpy as jnp
import numpy as np
from jax import lax
from jax.experimental import pallas as pl
from jax.experimental.pallas import tpu as pltpu
from jax.sharding import PartitionSpec as P

EPS = 1e-05
TINY = 1e-06
LANES = 128
INNER = 128
OCTET = 8
f32 = jnp.float32
bf16 = jnp.bfloat16


def first_stage(outer, level):
    part = outer >> level
    index = np.arange(part)
    angle = (index[:, None] + 0.5) * index[None, :] * (math.pi / part)
    block = np.stack([np.cos(angle), -np.sin(angle)], 1).reshape(2 * part, part)
    return np.kron(np.eye(1 << level), block)


def turn_table(outer, level):
    part = outer >> level
    index = np.arange(outer) % part
    angle = (index[:, None] + 0.5) * np.arange(INNER)[None, :] * (math.pi / (part * INNER))
    return np.stack([np.cos(angle), np.sin(angle)])


def conv_tables(bin_rows, bucket, limits):
    outer = bin_rows // INNER
    levels = range(3)
    eye = np.eye(OCTET)
    firsts = [first_stage(outer, n) for n in levels]
    ones = np.stack([np.kron(item, eye) for item in firsts])
    backs = np.stack([np.kron(firsts[n].T / (bin_rows >> n), eye) for n in levels])
    turns = np.stack([turn_table(outer, n) for n in levels])
    inner_angle = (np.arange(INNER)[:, None] * np.arange(INNER)[None, :] % INNER) * (
        2.0 * math.pi / INNER
    )
    stage_one = jnp.asarray(ones, bf16)[bucket]
    back_one = jnp.asarray(backs, bf16)[bucket]
    turn = jnp.asarray(turns, f32)[bucket]
    base_c = jnp.asarray(np.cos(inner_angle), f32)
    base_s = jnp.asarray(np.sin(inner_angle), f32)
    cos_l = base_c[None] * turn[0][:, None, :] - base_s[None] * turn[1][:, None, :]
    sin_l = base_s[None] * turn[0][:, None, :] + base_c[None] * turn[1][:, None, :]
    stage_two = jnp.concatenate(
        [jnp.concatenate([cos_l, sin_l], 2), jnp.concatenate([-sin_l, cos_l], 2)], 1
    ).astype(bf16)
    cos_t = base_c[None] * turn[0][:, :, None] - base_s[None] * turn[1][:, :, None]
    sin_t = base_s[None] * turn[0][:, :, None] + base_c[None] * turn[1][:, :, None]
    back_two = jnp.concatenate(
        [jnp.concatenate([cos_t, -sin_t], 2), jnp.concatenate([sin_t, cos_t], 2)], 1
    ).astype(bf16)
    part = jnp.right_shift(jnp.int32(outer), bucket)
    chunk = jnp.arange(outer, dtype=jnp.int32)
    slot = chunk // part
    within = chunk - slot * part
    limit = jnp.sum(
        jnp.where(slot[:, None] == jnp.arange(limits.shape[0])[None, :], limits[None, :], 0), 1
    )
    room = jnp.broadcast_to((limit - within * INNER)[:, None], (outer, LANES)).astype(jnp.int32)
    joined = jnp.concatenate([(within > 0).astype(f32), jnp.zeros((OCTET,), f32)])
    joined = jnp.broadcast_to(joined[:, None], (outer + OCTET, LANES))
    same = (slot[:, None] == slot[None, :]).astype(f32)
    return (stage_one, stage_two, back_two, back_one, room, joined, same)


def shifted_back(now, before, iota):
    one = jnp.where(iota == 0, before[15:16], pltpu.roll(now, 1, 0))
    two = jnp.where(
        iota == 0, before[14:15], jnp.where(iota == 1, before[15:16], pltpu.roll(now, 2, 0))
    )
    return (one, two)


def load_chunk(ref, chunk, joined_row):
    now = ref[pl.ds(pl.multiple_of(chunk * INNER, INNER), INNER), :].astype(f32)
    at = pl.multiple_of(jnp.maximum(chunk * INNER - 16, 0), 16)
    before = ref[pl.ds(at, 16), :].astype(f32) * joined_row
    return (now, before)


def conv_forward_kernel(
    kern_ref, val_ref, taps_k, taps_v, one_ref, two_ref, back_two_ref, back_one_ref,
    room_ref, joined_ref, same_ref,
    out_ref, unit_ref, vspec_ref, norm_ref,
    time_buf, mid_buf, low_buf, square_buf,
):
    outer = kern_ref.shape[0] // INNER
    iota = lax.broadcasted_iota(jnp.int32, (INNER, LANES), 0)

    def prepare(chunk, carry):
        joined = joined_ref[pl.ds(chunk, 1), :]
        valid = iota < room_ref[pl.ds(chunk, 1), :]
        now, before = load_chunk(kern_ref, chunk, joined)
        one, two = shifted_back(now, before, iota)
        kern = jnp.where(valid, taps_k[0:1] * now + taps_k[1:2] * one + taps_k[2:3] * two, 0.0)
        time_buf[chunk, :, 0:LANES] = kern
        square_buf[pl.ds(chunk, 1), :] = jnp.sum(kern * kern, 0, keepdims=True)
        now, before = load_chunk(val_ref, chunk, joined)
        one, two = shifted_back(now, before, iota)
        val = jnp.where(valid, taps_v[0:1] * now + taps_v[1:2] * one + taps_v[2:3] * two, 0.0)
        time_buf[chunk, :, LANES:] = val
        return carry

    lax.fori_loop(0, outer, prepare, 0)
    total = jnp.dot(same_ref[...], square_buf[...], precision=lax.Precision.HIGHEST)
    norm = jnp.sqrt(total + TINY)
    norm_ref[...] = norm
    square_buf[...] = 1.0 / norm

    def stage_one(pair, carry):
        at = pl.multiple_of(pair * 16, 16)
        halves = []
        for half in range(2):
            part = time_buf[:, pl.ds(at + half * OCTET, OCTET), :]
            part = part.reshape(outer * OCTET, 2 * LANES).astype(bf16)
            done = jnp.dot(one_ref[...], part, preferred_element_type=f32)
            halves.append(done.reshape(2 * outer, OCTET, 2 * LANES))
        mid_buf[:, pl.ds(at, 16), :] = jnp.concatenate(halves, 1).astype(bf16)
        return carry

    lax.fori_loop(0, INNER // 16, stage_one, 0)

    def stage_two(kk, carry):
        row = pl.multiple_of(kk * 2, 2)
        part = mid_buf[pl.ds(row, 2)].reshape(2 * INNER, 2 * LANES)
        spec = jnp.dot(two_ref[kk], part, preferred_element_type=f32)
        inverse = square_buf[pl.ds(kk, 1), :]
        unit_re = spec[:INNER, :LANES] * inverse
        unit_im = spec[INNER:, :LANES] * inverse
        val_re = spec[:INNER, LANES:]
        val_im = spec[INNER:, LANES:]
        unit_ref[row] = unit_re.astype(bf16)
        unit_ref[row + 1] = unit_im.astype(bf16)
        vspec_ref[row] = val_re.astype(bf16)
        vspec_ref[row + 1] = val_im.astype(bf16)
        power = unit_re * unit_re + unit_im * unit_im
        made = jnp.concatenate([power * val_re, power * val_im], 0).astype(bf16)
        back = jnp.dot(back_two_ref[kk], made, preferred_element_type=f32)
        low_buf[row] = back[:INNER]
        low_buf[row + 1] = back[INNER:]
        return carry

    lax.fori_loop(0, outer, stage_two, 0, unroll=2)
    spot = lax.broadcasted_iota(jnp.int32, (outer, 16, LANES), 1)

    def back_one(pair, carry):
        at = pl.multiple_of(pair * 16, 16)
        halves = []
        for half in range(2):
            part = low_buf[:, pl.ds(at + half * OCTET, OCTET), :]
            part = part.reshape(2 * outer * OCTET, LANES).astype(bf16)
            done = jnp.dot(back_one_ref[...], part, preferred_element_type=f32)
            halves.append(done.reshape(outer, OCTET, LANES))
        whole = jnp.concatenate(halves, 1)
        valid = spot + at < room_ref[...][:, None, :]
        out_ref[:, pl.ds(at, 16), :] = jnp.where(valid, whole, 0.0).astype(bf16)
        return carry

    lax.fori_loop(0, INNER // 16, back_one, 0)


def conv_backward_kernel(
    grad_ref, kern_ref, val_ref, unit_ref, vspec_ref, norm_ref, taps_k, taps_v,
    one_ref, two_ref, back_two_ref, back_one_ref, room_ref, joined_ref, same_ref,
    dkern_ref, dval_ref, dtaps_k, dtaps_v,
    time_buf, mid_buf, low_buf, dots_buf, inv_buf,
):
    outer = kern_ref.shape[0] // INNER
    iota = lax.broadcasted_iota(jnp.int32, (INNER, LANES), 0)
    spot = lax.broadcasted_iota(jnp.int32, (outer, 16, LANES), 1)

    def stage_one(pair, carry):
        at = pl.multiple_of(pair * 16, 16)
        whole = grad_ref[:, pl.ds(at, 16), :].astype(f32)
        whole = jnp.where(spot + at < room_ref[...][:, None, :], whole, 0.0)
        halves = []
        for half in range(2):
            part = whole[:, half * OCTET : (half + 1) * OCTET]
            part = part.reshape(outer * OCTET, LANES).astype(bf16)
            done = jnp.dot(one_ref[...], part, preferred_element_type=f32)
            halves.append(done.reshape(2 * outer, OCTET, LANES))
        mid_buf[:, pl.ds(at, 16), :] = jnp.concatenate(halves, 1).astype(bf16)
        return carry

    lax.fori_loop(0, INNER // 16, stage_one, 0)

    def stage_two(kk, carry):
        row = pl.multiple_of(kk * 2, 2)
        part = mid_buf[pl.ds(row, 2)].reshape(2 * INNER, LANES)
        spec = jnp.dot(two_ref[kk], part, preferred_element_type=f32)
        grad_re = spec[:INNER]
        grad_im = spec[INNER:]
        unit_re = unit_ref[row].astype(f32)
        unit_im = unit_ref[row + 1].astype(f32)
        val_re = vspec_ref[row].astype(f32)
        val_im = vspec_ref[row + 1].astype(f32)
        power = unit_re * unit_re + unit_im * unit_im
        slope = 2.0 * (grad_re * val_re + grad_im * val_im)
        dots_buf[pl.ds(kk, 1), :] = jnp.sum(power * slope, 0, keepdims=True)
        upper = jnp.concatenate([power * grad_re, slope * unit_re], 1)
        lower = jnp.concatenate([power * grad_im, slope * unit_im], 1)
        made = jnp.concatenate([upper, lower], 0).astype(bf16)
        back = jnp.dot(back_two_ref[kk], made, preferred_element_type=f32)
        low_buf[row] = back[:INNER]
        low_buf[row + 1] = back[INNER:]
        return carry

    lax.fori_loop(0, outer, stage_two, 0, unroll=2)

    def back_one(octet, carry):
        at = pl.multiple_of(octet * OCTET, OCTET)
        part = low_buf[:, pl.ds(at, OCTET), :]
        part = part.reshape(2 * outer * OCTET, 2 * LANES).astype(bf16)
        done = jnp.dot(back_one_ref[...], part, preferred_element_type=f32)
        time_buf[:, pl.ds(at, OCTET), :] = done.reshape(outer, OCTET, 2 * LANES)
        return carry

    lax.fori_loop(0, INNER // OCTET, back_one, 0)
    inv_buf[...] = 1.0 / norm_ref[...]
    same = same_ref[...]
    share = same / (jnp.sum(same, 1, keepdims=True) * INNER)
    dots_buf[...] = jnp.dot(share, dots_buf[...], precision=lax.Precision.HIGHEST)

    def shifted_ahead(now, after):
        one = jnp.where(iota == INNER - 1, after[0:1], pltpu.roll(now, INNER - 1, 0))
        two = jnp.where(
            iota == INNER - 1,
            after[1:2],
            jnp.where(iota == INNER - 2, after[0:1], pltpu.roll(now, INNER - 2, 0)),
        )
        return (one, two)

    def finish(step, carry):
        after_k, after_v, sums = carry
        chunk = outer - 1 - step
        joined = joined_ref[pl.ds(chunk, 1), :]
        ahead = joined_ref[pl.ds(chunk + 1, 1), :]
        valid = iota < room_ref[pl.ds(chunk, 1), :]
        inverse = inv_buf[pl.ds(chunk, 1), :]
        along = dots_buf[pl.ds(chunk, 1), :]
        rows = pl.ds(pl.multiple_of(chunk * INNER, INNER), INNER)
        now, before = load_chunk(kern_ref, chunk, joined)
        one, two = shifted_back(now, before, iota)
        unit = (taps_k[0:1] * now + taps_k[1:2] * one + taps_k[2:3] * two) * inverse
        grad = jnp.where(valid, (time_buf[chunk, :, LANES:] - unit * along) * inverse, 0.0)
        ahead_one, ahead_two = shifted_ahead(grad, after_k * ahead)
        dkern_ref[rows, :] = (
            taps_k[0:1] * grad + taps_k[1:2] * ahead_one + taps_k[2:3] * ahead_two
        ).astype(bf16)
        made = [jnp.sum(grad * item, 0, keepdims=True) for item in (now, one, two)]
        after_k = grad[:OCTET]
        now, before = load_chunk(val_ref, chunk, joined)
        one, two = shifted_back(now, before, iota)
        grad = jnp.where(valid, time_buf[chunk, :, :LANES], 0.0)
        ahead_one, ahead_two = shifted_ahead(grad, after_v * ahead)
        dval_ref[rows, :] = (
            taps_v[0:1] * grad + taps_v[1:2] * ahead_one + taps_v[2:3] * ahead_two
        ).astype(bf16)
        made += [jnp.sum(grad * item, 0, keepdims=True) for item in (now, one, two)]
        after_v = grad[:OCTET]
        return (after_k, after_v, tuple(a + b for a, b in zip(sums, made)))

    zero = jnp.zeros((OCTET, LANES), f32)
    start = (zero, zero, tuple(jnp.zeros((1, LANES), f32) for _ in range(6)))
    _, _, sums = lax.fori_loop(0, outer, finish, start)
    for index in range(3):
        dtaps_k[index : index + 1, :] = sums[index]
        dtaps_v[index : index + 1, :] = sums[3 + index]


def whole_spec(shape):
    return pl.BlockSpec(shape, lambda c: (0,) * len(shape), pipeline_mode=pl.Buffered(1))


def lane_spec(rows):
    return pl.BlockSpec((rows, LANES), lambda c: (0, c))


def cube_spec(depth, rows):
    return pl.BlockSpec((depth, rows, LANES), lambda c: (0, 0, c))


def conv_forward(kern, val, taps_k, taps_v, tables):
    bin_rows, channels = kern.shape
    outer = bin_rows // INNER
    out, unit, vspec, norm = pl.pallas_call(
        conv_forward_kernel,
        grid=(channels // LANES,),
        in_specs=[lane_spec(bin_rows), lane_spec(bin_rows), lane_spec(3), lane_spec(3)]
        + [whole_spec(item.shape) for item in tables],
        out_specs=[
            cube_spec(outer, INNER),
            cube_spec(2 * outer, INNER),
            cube_spec(2 * outer, INNER),
            lane_spec(outer),
        ],
        out_shape=[
            jax.ShapeDtypeStruct((outer, INNER, channels), bf16),
            jax.ShapeDtypeStruct((2 * outer, INNER, channels), bf16),
            jax.ShapeDtypeStruct((2 * outer, INNER, channels), bf16),
            jax.ShapeDtypeStruct((outer, channels), f32),
        ],
        scratch_shapes=[
            pltpu.VMEM((outer, INNER, 2 * LANES), f32),
            pltpu.VMEM((2 * outer, INNER, 2 * LANES), bf16),
            pltpu.VMEM((2 * outer, INNER, LANES), f32),
            pltpu.VMEM((outer, LANES), f32),
        ],
        compiler_params=pltpu.CompilerParams(vmem_limit_bytes=56 << 20),
        cost_estimate=pl.CostEstimate(
            flops=26 * channels * bin_rows * 512, bytes_accessed=30 * bin_rows * channels, transcendentals=0
        ),
        name="conv_forward",
    )(kern, val, taps_k, taps_v, *tables)
    return (out.reshape(bin_rows, channels), unit, vspec, norm)


def conv_backward(grad, kern, val, unit, vspec, norm, taps_k, taps_v, tables):
    bin_rows, channels = kern.shape
    outer = bin_rows // INNER
    return pl.pallas_call(
        conv_backward_kernel,
        grid=(channels // LANES,),
        in_specs=[
            cube_spec(outer, INNER), lane_spec(bin_rows), lane_spec(bin_rows),
            cube_spec(2 * outer, INNER), cube_spec(2 * outer, INNER), lane_spec(outer),
            lane_spec(3), lane_spec(3),
        ]
        + [whole_spec(item.shape) for item in tables],
        out_specs=[lane_spec(bin_rows), lane_spec(bin_rows), lane_spec(3), lane_spec(3)],
        out_shape=[
            jax.ShapeDtypeStruct((bin_rows, channels), bf16),
            jax.ShapeDtypeStruct((bin_rows, channels), bf16),
            jax.ShapeDtypeStruct((3, channels), f32),
            jax.ShapeDtypeStruct((3, channels), f32),
        ],
        scratch_shapes=[
            pltpu.VMEM((outer, INNER, 2 * LANES), f32),
            pltpu.VMEM((2 * outer, INNER, LANES), bf16),
            pltpu.VMEM((2 * outer, INNER, 2 * LANES), f32),
            pltpu.VMEM((outer, LANES), f32),
            pltpu.VMEM((outer, LANES), f32),
        ],
        compiler_params=pltpu.CompilerParams(vmem_limit_bytes=56 << 20),
        cost_estimate=pl.CostEstimate(
            flops=30 * channels * bin_rows * 512, bytes_accessed=40 * bin_rows * channels, transcendentals=0
        ),
        name="conv_backward",
    )(grad.reshape(outer, INNER, channels), kern, val, unit, vspec, norm, taps_k, taps_v, *tables)


def norm_parts(values, gain, bias):
    row_mean = jnp.mean(values, -1, keepdims=True)
    centred = values - row_mean
    row_var = jnp.mean(centred * centred, -1, keepdims=True)
    inverse = lax.rsqrt(row_var + EPS)
    normed = centred * inverse
    return (normed * gain + bias, normed, inverse)


def norm_back(grad_out, normed, inverse, gain):
    scaled = grad_out * gain
    centre_term = jnp.mean(scaled, -1, keepdims=True)
    slope_term = jnp.mean(scaled * normed, -1, keepdims=True)
    return inverse * (scaled - centre_term - normed * slope_term)


def pad_lanes(array):
    extra = -array.shape[-1] % LANES
    if extra == 0:
        return array
    return jnp.pad(array, ((0, 0),) * (array.ndim - 1) + ((0, extra),))


def on_device(
    activations,
    cotangent,
    buckets,
    lengths,
    first_gain,
    first_bias,
    in_weight,
    in_bias,
    short_kernel,
    short_value,
    out_weight,
    out_bias,
    second_gain,
    second_bias,
    gate_weight,
    up_weight,
    down_weight,
):
    width = activations.shape[1]
    both = ("batch", "tensor")
    shard_rows = in_weight.shape[0]
    small = jnp.concatenate(
        [
            first_gain[:, None],
            first_bias[:, None],
            out_bias[:, None],
            second_gain[:, None],
            second_bias[:, None],
            short_kernel.T,
            short_value.T,
            in_bias.reshape(shard_rows, 3),
        ],
        1,
    )
    mixer = lax.all_gather(
        jnp.concatenate([in_weight, out_weight, pad_lanes(small)], 1), both, axis=0, tiled=True
    )
    in_full = mixer[:, : 3 * width]
    out_full = mixer[:, 3 * width : 4 * width]
    rows_small = mixer[:, 4 * width : 4 * width + 14].astype(f32).T
    gain_one, bias_one, out_shift, gain_two, bias_two = (rows_small[n] for n in range(5))
    taps_kernel = rows_small[5:8]
    taps_value = rows_small[8:11]
    in_shift = rows_small[11:14].T.reshape(3 * width)
    shards = (
        lax.all_gather(gate_weight, "batch", axis=0, tiled=True),
        lax.all_gather(up_weight, "batch", axis=0, tiled=True),
        lax.all_gather(down_weight, "batch", axis=1, tiled=True),
    )
    rows_in = activations.astype(f32)
    first_out, first_hat, first_inv = norm_parts(rows_in, gain_one, bias_one)
    normed_first = first_out.astype(bf16)
    projected = jnp.dot(normed_first, in_full, preferred_element_type=f32) + in_shift
    queries = projected[:, :width]
    kernels, values = (
        lax.all_to_all(
            projected[:, n * width : (n + 1) * width].astype(bf16),
            "tensor",
            split_axis=1,
            concat_axis=0,
            tiled=True,
        )
        for n in (1, 2)
    )
    bin_rows, channels = kernels.shape
    chan_start = lax.axis_index("tensor") * channels
    short_k = pad_lanes(lax.dynamic_slice_in_dim(taps_kernel, chan_start, channels, 1))
    short_v = pad_lanes(lax.dynamic_slice_in_dim(taps_value, chan_start, channels, 1))
    kernels = pad_lanes(kernels)
    values = pad_lanes(values)
    bucket_here = buckets[lax.axis_index("batch")]
    tables = conv_tables(bin_rows, bucket_here, lengths[0])
    mixed_chan, unit_spec, value_spec, norms = conv_forward(
        kernels, values, short_k, short_v, tables
    )
    norm_part = jnp.sum(norms[:, :channels], 0) / (bin_rows // INNER) * jnp.left_shift(
        jnp.int32(1), bucket_here
    ).astype(f32)
    mixed = lax.all_to_all(
        mixed_chan[:, :channels], "tensor", split_axis=0, concat_axis=1, tiled=True
    ).astype(f32)
    gated = (queries * mixed).astype(bf16)
    middle = rows_in + jnp.dot(gated, out_full, preferred_element_type=f32) + out_shift
    second_out, second_hat, second_inv = norm_parts(middle, gain_two, bias_two)
    normed_second = second_out.astype(bf16)
    full_weights = (
        lax.all_gather(shards[0], "tensor", axis=1, tiled=True),
        lax.all_gather(shards[1], "tensor", axis=1, tiled=True),
        lax.all_gather(shards[2], "tensor", axis=0, tiled=True),
    )
    gate_pre = jnp.dot(normed_second, full_weights[0], preferred_element_type=f32)
    up_value = jnp.dot(normed_second, full_weights[1], preferred_element_type=f32)
    gate_sigmoid = jax.nn.sigmoid(gate_pre)
    gate_silu = gate_pre * gate_sigmoid
    hidden = (gate_silu * up_value).astype(bf16)
    out_rows = middle + jnp.dot(hidden, full_weights[2], preferred_element_type=f32)
    cot_low = cotangent.astype(bf16)
    d_hidden = jnp.einsum("rd,fd->rf", cot_low, full_weights[2], preferred_element_type=f32)
    down_whole = jnp.einsum("rf,rd->fd", hidden, cot_low, preferred_element_type=f32)
    d_up = (d_hidden * gate_silu).astype(bf16)
    d_gate = (d_hidden * up_value * gate_sigmoid * (1.0 + gate_pre * (1.0 - gate_sigmoid))).astype(
        bf16
    )
    gate_whole = jnp.einsum("rd,rf->df", normed_second, d_gate, preferred_element_type=f32)
    up_whole = jnp.einsum("rd,rf->df", normed_second, d_up, preferred_element_type=f32)
    d_second = jnp.einsum(
        "rf,df->rd", d_gate, full_weights[0], preferred_element_type=f32
    ) + jnp.einsum("rf,df->rd", d_up, full_weights[1], preferred_element_type=f32)
    mlp_summed = tuple(
        lax.psum_scatter(
            lax.psum_scatter(
                grad.astype(bf16), "tensor", scatter_dimension=1 - dim, tiled=True
            ),
            "batch",
            scatter_dimension=dim,
            tiled=True,
        ).astype(f32)
        for grad, dim in ((gate_whole, 0), (up_whole, 0), (down_whole, 1))
    )
    grad_middle = cotangent + norm_back(d_second, second_hat, second_inv, gain_two)
    grad_gain_two = jnp.sum(d_second * second_hat, 0)
    grad_bias_two = jnp.sum(d_second, 0)
    d_mix = grad_middle.astype(bf16)
    grad_out_full = jnp.einsum("rd,re->de", gated, d_mix, preferred_element_type=f32)
    grad_out_shift = jnp.sum(d_mix.astype(f32), 0)
    d_gated = jnp.einsum("re,de->rd", d_mix, out_full, preferred_element_type=f32)
    d_queries = d_gated * mixed
    d_mixed = (d_gated * queries).astype(bf16)
    d_mixed_chan = lax.all_to_all(d_mixed, "tensor", split_axis=1, concat_axis=0, tiled=True)
    d_kernels, d_values, d_taps_k, d_taps_v = conv_backward(
        pad_lanes(d_mixed_chan), kernels, values, unit_spec, value_spec, norms,
        short_k, short_v, tables,
    )
    d_kernel_rows, d_value_rows = (
        lax.all_to_all(item[:, :channels], "tensor", split_axis=0, concat_axis=1, tiled=True)
        for item in (d_kernels, d_values)
    )
    d_projected = jnp.concatenate([d_queries.astype(bf16), d_kernel_rows, d_value_rows], 1)
    grad_in_full = jnp.einsum("rd,rk->dk", normed_first, d_projected, preferred_element_type=f32)
    grad_in_shift = jnp.sum(d_projected.astype(f32), 0)
    d_first = jnp.einsum("rk,dk->rd", d_projected, in_full, preferred_element_type=f32)
    grad_activations = grad_middle + norm_back(d_first, first_hat, first_inv, gain_one)
    grad_gain_one = jnp.sum(d_first * first_hat, 0)
    grad_bias_one = jnp.sum(d_first, 0)
    chan_rows = jnp.concatenate(
        [d_taps_k[:, :channels], d_taps_v[:, :channels], norm_part[None]], 0
    )
    chan_full = lax.dynamic_update_slice(
        jnp.zeros((7, width), f32), chan_rows, (jnp.int32(0), chan_start)
    )
    small_rows = jnp.concatenate(
        [
            grad_gain_one[None],
            grad_bias_one[None],
            grad_out_shift[None],
            grad_gain_two[None],
            grad_bias_two[None],
            chan_full,
            grad_in_shift.reshape(width, 3).T,
        ],
        0,
    )
    small_sum = lax.psum_scatter(
        pad_lanes(small_rows.T), both, scatter_dimension=0, tiled=True
    )
    mixer_sum = lax.psum_scatter(
        jnp.concatenate([grad_in_full.astype(bf16), grad_out_full.astype(bf16)], 1),
        both,
        scatter_dimension=0,
        tiled=True,
    ).astype(f32)
    seq_count = jnp.sum(jnp.left_shift(jnp.ones_like(buckets), buckets)).astype(f32)
    return (
        out_rows,
        grad_activations,
        small_sum[:, 0],
        small_sum[:, 1],
        mixer_sum[:, : 3 * width],
        small_sum[:, 12:15].reshape(3 * shard_rows),
        small_sum[:, 5:8].T,
        small_sum[:, 8:11].T,
        mixer_sum[:, 3 * width :],
        small_sum[:, 2],
        small_sum[:, 3],
        small_sum[:, 4],
        mlp_summed[0],
        mlp_summed[1],
        mlp_summed[2],
        small_sum[:, 11] / seq_count,
    )


def solution(mesh):
    return jax.shard_map(
        on_device,
        mesh=mesh,
        in_specs=(
            P(("batch", "tensor"), None),
            P(("batch", "tensor"), None),
            P(),
            P("batch", None),
            P(("batch", "tensor")),
            P(("batch", "tensor")),
            P(("batch", "tensor"), None),
            P(("batch", "tensor")),
            P(None, ("batch", "tensor")),
            P(None, ("batch", "tensor")),
            P(("batch", "tensor"), None),
            P(("batch", "tensor")),
            P(("batch", "tensor")),
            P(("batch", "tensor")),
            P("batch", "tensor"),
            P("batch", "tensor"),
            P("tensor", "batch"),
        ),
        out_specs=(
            P(("batch", "tensor"), None),
            P(("batch", "tensor"), None),
            P(("batch", "tensor")),
            P(("batch", "tensor")),
            P(("batch", "tensor"), None),
            P(("batch", "tensor")),
            P(None, ("batch", "tensor")),
            P(None, ("batch", "tensor")),
            P(("batch", "tensor"), None),
            P(("batch", "tensor")),
            P(("batch", "tensor")),
            P(("batch", "tensor")),
            P("batch", "tensor"),
            P("batch", "tensor"),
            P("tensor", "batch"),
            P(("batch", "tensor")),
        ),
        check_vma=False,
    )
```

```python
import functools
import math

import jax
import jax.numpy as jnp
import numpy as np
from jax import lax
from jax.experimental import pallas as pl
from jax.experimental.pallas import tpu as pltpu
from jax.sharding import PartitionSpec as P

EPS = 1e-05
TINY = 1e-06
LANES = 128
INNER = 128
OCTET = 8
f32 = jnp.float32
bf16 = jnp.bfloat16


def first_stage(outer, level):
    part = outer >> level
    index = np.arange(part)
    angle = (index[:, None] + 0.5) * index[None, :] * (math.pi / part)
    block = np.stack([np.cos(angle), -np.sin(angle)], 1).reshape(2 * part, part)
    return np.kron(np.eye(1 << level), block)


def turn_angles(outer, level):
    part = outer >> level
    index = np.arange(outer) % part
    return (index[:, None] + 0.5) * np.arange(INNER)[None, :] * (math.pi / (part * INNER))


def conv_tables(bin_rows):
    outer = bin_rows // INNER
    eye = np.eye(OCTET)
    base = np.arange(INNER)[:, None] * np.arange(INNER)[None, :] % INNER * (2.0 * math.pi / INNER)
    ones, backs, twos, flips = ([], [], [], [])
    for level in range(3):
        first = first_stage(outer, level)
        ones.append(np.kron(first, eye))
        backs.append(np.kron(first.T / (bin_rows >> level), eye))
        angle = base[None] + turn_angles(outer, level)[:, None, :]
        upper = np.concatenate([np.cos(angle), np.sin(angle)], 2)
        lower = np.concatenate([-np.sin(angle), np.cos(angle)], 2)
        both = np.concatenate([upper, lower], 1)
        twos.append(both)
        flips.append(both.transpose(0, 2, 1))
    return tuple(
        jnp.asarray(np.stack(item).astype(np.float32).astype(bf16))
        for item in (ones, twos, flips, backs)
    )


def lay_out(meta, room_ref, joined_ref, count):
    outer = room_ref.shape[0]
    shift = int(math.log2(outer)) - meta[0]

    def row(chunk, carry):
        slot = lax.shift_right_logical(chunk, shift)
        within = chunk - lax.shift_left(slot, shift)
        room = meta[1 + count + slot] - within * INNER
        room_ref[pl.ds(chunk, 1), :] = jnp.full((1, LANES), room, jnp.int32)
        joined_ref[pl.ds(chunk, 1), :] = jnp.full((1, LANES), jnp.minimum(within, 1)).astype(f32)
        return carry

    lax.fori_loop(0, outer, row, 0)
    joined_ref[outer:, :] = jnp.zeros((OCTET, LANES), f32)
    left = lax.broadcasted_iota(jnp.int32, (outer, outer), 0)
    right = lax.broadcasted_iota(jnp.int32, (outer, outer), 1)
    same = lax.shift_right_logical(left, shift) == lax.shift_right_logical(right, shift)
    return same.astype(f32)


def shifted_back(now, before, iota):
    one = jnp.where(iota == 0, before[15:16], pltpu.roll(now, 1, 0))
    two = jnp.where(
        iota == 0, before[14:15], jnp.where(iota == 1, before[15:16], pltpu.roll(now, 2, 0))
    )
    return (one, two)


def load_chunk(ref, chunk, joined_row):
    now = ref[pl.ds(pl.multiple_of(chunk * INNER, INNER), INNER), :].astype(f32)
    at = pl.multiple_of(jnp.maximum(chunk * INNER - 16, 0), 16)
    before = ref[pl.ds(at, 16), :].astype(f32) * joined_row
    return (now, before)


def fill_rows(meta, pieces, target):
    rows = pieces[0].shape[0]
    for index, piece in enumerate(pieces):
        at = pl.multiple_of(meta[1 + index] * rows, rows)
        target[pl.ds(at, rows), :] = piece[...]


def conv_forward_kernel(
    count, meta, *refs
):
    kern_pieces, val_pieces, refs = (refs[:count], refs[count : 2 * count], refs[2 * count :])
    conv_forward_body(meta, kern_pieces, val_pieces, refs[6 : 6 + count], *refs[:6], *refs[6 + count :])


def conv_forward_body(
    meta, kern_pieces, val_pieces, outs, taps_k, taps_v, one_ref, two_ref, back_two_ref,
    back_one_ref,
    unit_ref, vspec_ref, norm_ref,
    kern_ref, val_ref, time_buf, mid_buf, low_buf, square_buf, room_ref, joined_ref,
):
    outer = kern_ref.shape[0] // INNER
    count = len(kern_pieces)
    same = lay_out(meta, room_ref, joined_ref, count)
    fill_rows(meta, kern_pieces, kern_ref)
    fill_rows(meta, val_pieces, val_ref)
    iota = lax.broadcasted_iota(jnp.int32, (INNER, LANES), 0)

    def prepare(chunk, carry):
        joined = joined_ref[pl.ds(chunk, 1), :]
        valid = iota < room_ref[pl.ds(chunk, 1), :]
        now, before = load_chunk(kern_ref, chunk, joined)
        one, two = shifted_back(now, before, iota)
        kern = jnp.where(valid, taps_k[0:1] * now + taps_k[1:2] * one + taps_k[2:3] * two, 0.0)
        time_buf[chunk, :, 0:LANES] = kern
        square_buf[pl.ds(chunk, 1), :] = jnp.sum(kern * kern, 0, keepdims=True)
        now, before = load_chunk(val_ref, chunk, joined)
        one, two = shifted_back(now, before, iota)
        val = jnp.where(valid, taps_v[0:1] * now + taps_v[1:2] * one + taps_v[2:3] * two, 0.0)
        time_buf[chunk, :, LANES:] = val
        return carry

    lax.fori_loop(0, outer, prepare, 0, unroll=4)
    total = jnp.dot(same, square_buf[...], precision=lax.Precision.HIGHEST)
    norm = jnp.sqrt(total + TINY)
    norm_ref[...] = norm
    square_buf[...] = 1.0 / norm

    def stage_one(pair, carry):
        at = pl.multiple_of(pair * 16, 16)
        halves = []
        for half in range(2):
            part = time_buf[:, pl.ds(at + half * OCTET, OCTET), :]
            part = part.reshape(outer * OCTET, 2 * LANES).astype(bf16)
            done = jnp.dot(one_ref[0], part, preferred_element_type=f32)
            halves.append(done.reshape(2 * outer, OCTET, 2 * LANES))
        mid_buf[:, pl.ds(at, 16), :] = jnp.concatenate(halves, 1).astype(bf16)
        return carry

    lax.fori_loop(0, INNER // 16, stage_one, 0, unroll=8)

    def stage_two(kk, carry):
        row = pl.multiple_of(kk * 2, 2)
        part = mid_buf[pl.ds(row, 2)].reshape(2 * INNER, 2 * LANES)
        spec = jnp.dot(two_ref[0, kk], part, preferred_element_type=f32)
        inverse = square_buf[pl.ds(kk, 1), :]
        unit_re = spec[:INNER, :LANES] * inverse
        unit_im = spec[INNER:, :LANES] * inverse
        val_re = spec[:INNER, LANES:]
        val_im = spec[INNER:, LANES:]
        unit_ref[row] = unit_re.astype(bf16)
        unit_ref[row + 1] = unit_im.astype(bf16)
        vspec_ref[row] = val_re.astype(bf16)
        vspec_ref[row + 1] = val_im.astype(bf16)
        power = unit_re * unit_re + unit_im * unit_im
        made = jnp.concatenate([power * val_re, power * val_im], 0).astype(bf16)
        back = jnp.dot(back_two_ref[0, kk], made, preferred_element_type=f32)
        low_buf[row] = back[:INNER]
        low_buf[row + 1] = back[INNER:]
        return carry

    lax.fori_loop(0, outer, stage_two, 0, unroll=16)
    spot = lax.broadcasted_iota(jnp.int32, (outer, 16, LANES), 1)

    def back_one(pair, carry):
        at = pl.multiple_of(pair * 16, 16)
        halves = []
        for half in range(2):
            part = low_buf[:, pl.ds(at + half * OCTET, OCTET), :]
            part = part.reshape(2 * outer * OCTET, LANES).astype(bf16)
            done = jnp.dot(back_one_ref[0], part, preferred_element_type=f32)
            halves.append(done.reshape(outer, OCTET, LANES))
        whole = jnp.concatenate(halves, 1)
        valid = spot + at < room_ref[...][:, None, :]
        whole = jnp.where(valid, whole, 0.0).astype(bf16)
        part = outer // count
        for index in range(count):
            for role in range(count):

                @pl.when(meta[1 + index] == role)
                def _(index=index, role=role):
                    outs[role][:, pl.ds(at, 16), :] = whole[index * part : (index + 1) * part]

        return carry

    lax.fori_loop(0, INNER // 16, back_one, 0, unroll=8)


def conv_backward_kernel(count, meta, *refs):
    groups = [refs[n * count : (n + 1) * count] for n in range(3)]
    refs = refs[3 * count :]
    conv_backward_body(meta, *groups, refs[9 : 9 + count], *refs[:9], *refs[9 + count :])


def conv_backward_body(
    meta, grad_pieces, kern_pieces, val_pieces, outs, unit_ref, vspec_ref, norm_ref, taps_k, taps_v,
    one_ref, two_ref, back_two_ref, back_one_ref,
    dtaps_k, dtaps_v,
    kern_ref, val_ref, grad_buf, time_buf, mid_buf, low_buf, dots_buf, inv_buf,
    room_ref, joined_ref,
):
    outer = kern_ref.shape[0] // INNER
    count = len(kern_pieces)
    same = lay_out(meta, room_ref, joined_ref, count)
    part = outer // count
    fill_rows(meta, kern_pieces, kern_ref)
    fill_rows(meta, val_pieces, val_ref)
    for index, piece in enumerate(grad_pieces):
        grad_buf[pl.ds(meta[1 + index] * part, part)] = piece[...]
    iota = lax.broadcasted_iota(jnp.int32, (INNER, LANES), 0)
    spot = lax.broadcasted_iota(jnp.int32, (outer, 16, LANES), 1)

    def stage_one(pair, carry):
        at = pl.multiple_of(pair * 16, 16)
        whole = grad_buf[:, pl.ds(at, 16), :].astype(f32)
        whole = jnp.where(spot + at < room_ref[...][:, None, :], whole, 0.0)
        halves = []
        for half in range(2):
            part = whole[:, half * OCTET : (half + 1) * OCTET]
            part = part.reshape(outer * OCTET, LANES).astype(bf16)
            done = jnp.dot(one_ref[0], part, preferred_element_type=f32)
            halves.append(done.reshape(2 * outer, OCTET, LANES))
        mid_buf[:, pl.ds(at, 16), :] = jnp.concatenate(halves, 1).astype(bf16)
        return carry

    lax.fori_loop(0, INNER // 16, stage_one, 0, unroll=8)

    def stage_two(kk, carry):
        row = pl.multiple_of(kk * 2, 2)
        part = mid_buf[pl.ds(row, 2)].reshape(2 * INNER, LANES)
        spec = jnp.dot(two_ref[0, kk], part, preferred_element_type=f32)
        grad_re = spec[:INNER]
        grad_im = spec[INNER:]
        unit_re = unit_ref[row].astype(f32)
        unit_im = unit_ref[row + 1].astype(f32)
        val_re = vspec_ref[row].astype(f32)
        val_im = vspec_ref[row + 1].astype(f32)
        power = unit_re * unit_re + unit_im * unit_im
        slope = 2.0 * (grad_re * val_re + grad_im * val_im)
        dots_buf[pl.ds(kk, 1), :] = jnp.sum(power * slope, 0, keepdims=True)
        upper = jnp.concatenate([power * grad_re, slope * unit_re], 1)
        lower = jnp.concatenate([power * grad_im, slope * unit_im], 1)
        made = jnp.concatenate([upper, lower], 0).astype(bf16)
        back = jnp.dot(back_two_ref[0, kk], made, preferred_element_type=f32)
        low_buf[row] = back[:INNER]
        low_buf[row + 1] = back[INNER:]
        return carry

    lax.fori_loop(0, outer, stage_two, 0, unroll=16)

    def back_one(octet, carry):
        at = pl.multiple_of(octet * OCTET, OCTET)
        part = low_buf[:, pl.ds(at, OCTET), :]
        part = part.reshape(2 * outer * OCTET, 2 * LANES).astype(bf16)
        done = jnp.dot(back_one_ref[0], part, preferred_element_type=f32)
        time_buf[:, pl.ds(at, OCTET), :] = done.reshape(outer, OCTET, 2 * LANES)
        return carry

    lax.fori_loop(0, INNER // OCTET, back_one, 0, unroll=16)
    inv_buf[...] = 1.0 / norm_ref[...]
    share = same / (jnp.sum(same, 1, keepdims=True) * INNER)
    dots_buf[...] = jnp.dot(share, dots_buf[...], precision=lax.Precision.HIGHEST)

    def shifted_ahead(now, after):
        one = jnp.where(iota == INNER - 1, after[0:1], pltpu.roll(now, INNER - 1, 0))
        two = jnp.where(
            iota == INNER - 1,
            after[1:2],
            jnp.where(iota == INNER - 2, after[0:1], pltpu.roll(now, INNER - 2, 0)),
        )
        return (one, two)

    def finish(step, carry):
        after_k, after_v, sums = carry
        chunk = outer - 1 - step
        joined = joined_ref[pl.ds(chunk, 1), :]
        ahead = joined_ref[pl.ds(chunk + 1, 1), :]
        valid = iota < room_ref[pl.ds(chunk, 1), :]
        inverse = inv_buf[pl.ds(chunk, 1), :]
        along = dots_buf[pl.ds(chunk, 1), :]
        slot = meta[1 + chunk // part]
        rows = pl.ds(pl.multiple_of(lax.rem(chunk, part) * INNER, INNER), INNER)
        now, before = load_chunk(kern_ref, chunk, joined)
        one, two = shifted_back(now, before, iota)
        unit = (taps_k[0:1] * now + taps_k[1:2] * one + taps_k[2:3] * two) * inverse
        grad = jnp.where(valid, (time_buf[chunk, :, LANES:] - unit * along) * inverse, 0.0)
        ahead_one, ahead_two = shifted_ahead(grad, after_k * ahead)
        d_kern = (
            taps_k[0:1] * grad + taps_k[1:2] * ahead_one + taps_k[2:3] * ahead_two
        ).astype(bf16)
        made = [jnp.sum(grad * item, 0, keepdims=True) for item in (now, one, two)]
        after_k = grad[:OCTET]
        now, before = load_chunk(val_ref, chunk, joined)
        one, two = shifted_back(now, before, iota)
        grad = jnp.where(valid, time_buf[chunk, :, :LANES], 0.0)
        ahead_one, ahead_two = shifted_ahead(grad, after_v * ahead)
        d_val = (
            taps_v[0:1] * grad + taps_v[1:2] * ahead_one + taps_v[2:3] * ahead_two
        ).astype(bf16)
        for role in range(count):

            @pl.when(slot == role)
            def _(role=role):
                outs[role][0, rows, :] = d_kern
                outs[role][1, rows, :] = d_val

        made += [jnp.sum(grad * item, 0, keepdims=True) for item in (now, one, two)]
        after_v = grad[:OCTET]
        return (after_k, after_v, tuple(a + b for a, b in zip(sums, made)))

    zero = jnp.zeros((OCTET, LANES), f32)
    start = (zero, zero, tuple(jnp.zeros((1, LANES), f32) for _ in range(6)))
    _, _, sums = lax.fori_loop(0, outer, finish, start, unroll=4)
    for index in range(3):
        dtaps_k[index : index + 1, :] = sums[index]
        dtaps_v[index : index + 1, :] = sums[3 + index]


def level_spec(shape):
    zeros = (0,) * (len(shape) - 1)
    return pl.BlockSpec(
        (1,) + shape[1:], lambda c, meta: (meta[0],) + zeros, pipeline_mode=pl.Buffered(1)
    )


def lane_spec(rows, start=0):
    return pl.BlockSpec((rows, LANES), lambda c, meta: (0, c + start))


def cube_spec(depth, rows):
    return pl.BlockSpec((depth, rows, LANES), lambda c, meta: (0, 0, c))


def conv_forward(pieces, meta, taps_k, taps_v, tables):
    count = len(pieces)
    rows, channels = pieces[0].shape[0], pieces[0].shape[1] // 2
    bin_rows = rows * count
    outer = bin_rows // INNER
    blocks = channels // LANES
    return pl.pallas_call(
        functools.partial(conv_forward_kernel, count),
        grid_spec=pltpu.PrefetchScalarGridSpec(
            num_scalar_prefetch=1,
            grid=(blocks,),
            in_specs=[lane_spec(rows)] * count
            + [lane_spec(rows, blocks)] * count
            + [lane_spec(3), lane_spec(3)]
            + [level_spec(item.shape) for item in tables],
            out_specs=[cube_spec(outer // count, INNER)] * count
            + [
                cube_spec(2 * outer, INNER),
                cube_spec(2 * outer, INNER),
                lane_spec(outer),
            ],
            scratch_shapes=[
                pltpu.VMEM((bin_rows, LANES), bf16),
                pltpu.VMEM((bin_rows, LANES), bf16),
                pltpu.VMEM((outer, INNER, 2 * LANES), f32),
                pltpu.VMEM((2 * outer, INNER, 2 * LANES), bf16),
                pltpu.VMEM((2 * outer, INNER, LANES), f32),
                pltpu.VMEM((outer, LANES), f32),
                pltpu.VMEM((outer, LANES), jnp.int32),
                pltpu.VMEM((outer + OCTET, LANES), f32),
            ],
        ),
        out_shape=[jax.ShapeDtypeStruct((outer // count, INNER, channels), bf16)] * count
        + [
            jax.ShapeDtypeStruct((2 * outer, INNER, channels), bf16),
            jax.ShapeDtypeStruct((2 * outer, INNER, channels), bf16),
            jax.ShapeDtypeStruct((outer, channels), f32),
        ],
        compiler_params=pltpu.CompilerParams(vmem_limit_bytes=56 << 20),
        cost_estimate=pl.CostEstimate(
            flops=26 * channels * bin_rows * 512,
            bytes_accessed=30 * bin_rows * channels,
            transcendentals=0,
        ),
        name="conv_forward",
    )(meta, *pieces, *pieces, taps_k, taps_v, *tables)


def conv_backward(grads, pieces, meta, unit, vspec, norm, taps_k, taps_v, tables):
    count = len(pieces)
    rows, channels = pieces[0].shape[0], pieces[0].shape[1] // 2
    bin_rows = rows * count
    outer = bin_rows // INNER
    blocks = channels // LANES
    part = outer // count
    rows_out = pl.BlockSpec((2, rows, LANES), lambda c, meta: (0, 0, c))
    return pl.pallas_call(
        functools.partial(conv_backward_kernel, count),
        grid_spec=pltpu.PrefetchScalarGridSpec(
            num_scalar_prefetch=1,
            grid=(blocks,),
            in_specs=[cube_spec(part, INNER)] * count
            + [lane_spec(rows)] * count
            + [lane_spec(rows, blocks)] * count
            + [cube_spec(2 * outer, INNER), cube_spec(2 * outer, INNER), lane_spec(outer)]
            + [lane_spec(3), lane_spec(3)]
            + [level_spec(item.shape) for item in tables],
            out_specs=[rows_out] * count + [lane_spec(3), lane_spec(3)],
            scratch_shapes=[
                pltpu.VMEM((bin_rows, LANES), bf16),
                pltpu.VMEM((bin_rows, LANES), bf16),
                pltpu.VMEM((outer, INNER, LANES), bf16),
                pltpu.VMEM((outer, INNER, 2 * LANES), f32),
                pltpu.VMEM((2 * outer, INNER, LANES), bf16),
                pltpu.VMEM((2 * outer, INNER, 2 * LANES), f32),
                pltpu.VMEM((outer, LANES), f32),
                pltpu.VMEM((outer, LANES), f32),
                pltpu.VMEM((outer, LANES), jnp.int32),
                pltpu.VMEM((outer + OCTET, LANES), f32),
            ],
        ),
        out_shape=[jax.ShapeDtypeStruct((2, rows, channels), bf16)] * count
        + [
            jax.ShapeDtypeStruct((3, channels), f32),
            jax.ShapeDtypeStruct((3, channels), f32),
        ],
        compiler_params=pltpu.CompilerParams(vmem_limit_bytes=56 << 20),
        cost_estimate=pl.CostEstimate(
            flops=channels * bin_rows,
            bytes_accessed=bin_rows * channels,
            transcendentals=0,
        ),
        name="conv_backward",
    )(
        meta,
        *(item.reshape(part, INNER, channels) for item in grads),
        *pieces,
        *pieces,
        unit,
        vspec,
        norm,
        taps_k,
        taps_v,
        *tables,
    )


def norm_parts(values, gain, bias):
    row_mean = jnp.mean(values, -1, keepdims=True)
    centred = values - row_mean
    row_var = jnp.mean(centred * centred, -1, keepdims=True)
    inverse = lax.rsqrt(row_var + EPS)
    normed = centred * inverse
    return (normed * gain + bias, normed, inverse)


def norm_back(grad_out, normed, inverse, gain):
    scaled = grad_out * gain
    centre_term = jnp.mean(scaled, -1, keepdims=True)
    slope_term = jnp.mean(scaled * normed, -1, keepdims=True)
    return inverse * (scaled - centre_term - normed * slope_term)


ROW_TILE = 1024
TURN = 256


def dot_nt(left, right):
    return lax.dot_general(left, right, (((1,), (1,)), ((), ())), preferred_element_type=f32)


def feed_kernel(
    normed_ref, cot_ref, gate_ref, up_ref, down_ref,
    out_ref, second_ref, packed_ref,
    normed_t, cot_t, sums,
):
    step = pl.program_id(0)
    rows = normed_ref.shape[0]
    tile = packed_ref.shape[-1]
    chunk = min(ROW_TILE, rows)

    @pl.when(step == 0)
    def _():
        out_ref[...] = jnp.zeros_like(out_ref)
        second_ref[...] = jnp.zeros_like(second_ref)

        def turn(index, carry):
            at = pl.multiple_of(index * TURN, TURN)
            normed_t[:, pl.ds(at, TURN)] = normed_ref[pl.ds(at, TURN), :].T
            cot_t[:, pl.ds(at, TURN)] = cot_ref[pl.ds(at, TURN), :].T
            return carry

        lax.fori_loop(0, rows // TURN, turn, 0)

    sums[...] = jnp.zeros_like(sums)

    def work(index, carry):
        at = pl.multiple_of(index * chunk, chunk)
        here = pl.ds(at, chunk)
        normed = normed_ref[here, :]
        cot = cot_ref[here, :]
        gate = jnp.dot(normed, gate_ref[0], preferred_element_type=f32)
        up = jnp.dot(normed, up_ref[0], preferred_element_type=f32)
        d_hidden = jnp.dot(cot, down_ref[0], preferred_element_type=f32)
        sigmoid = 1.0 / (1.0 + jnp.exp(-gate))
        silu = gate * sigmoid
        hidden = (silu * up).astype(bf16)
        d_up = (d_hidden * silu).astype(bf16)
        d_gate = (d_hidden * up * sigmoid * (1.0 + gate * (1.0 - sigmoid))).astype(bf16)
        out_ref[here, :] += dot_nt(hidden, down_ref[0])
        second_ref[here, :] += dot_nt(d_gate, gate_ref[0]) + dot_nt(d_up, up_ref[0])
        sums[0] += jnp.dot(normed_t[:, here], d_gate, preferred_element_type=f32)
        sums[1] += jnp.dot(normed_t[:, here], d_up, preferred_element_type=f32)
        sums[2] += jnp.dot(cot_t[:, here], hidden, preferred_element_type=f32)
        return carry

    lax.fori_loop(0, rows // chunk, work, 0)
    for kind in range(3):
        packed_ref[0, :, kind] = sums[kind].reshape(-1, *packed_ref.shape[3:]).astype(bf16)

def feed_forward(normed, cot, weights, hidden_cols, batch):
    rows, width = normed.shape
    parts = weights.shape[0]
    tile = 512 if hidden_cols % 512 == 0 else hidden_cols
    tiles = hidden_cols // tile

    def block(kind):
        return pl.BlockSpec((1, width, tile), lambda n: (n // tiles, 0, kind * tiles + n % tiles))
    whole = pl.BlockSpec((rows, width), lambda n: (0, 0), pipeline_mode=pl.Buffered(1))
    return pl.pallas_call(
        feed_kernel,
        grid=(parts * tiles,),
        in_specs=[whole, whole, block(0), block(1), block(2)],
        out_specs=[whole, whole, pl.BlockSpec((1, batch, 3, width // batch, tile), lambda n: (n // tiles, 0, 0, 0, n % tiles))],
        out_shape=[
            jax.ShapeDtypeStruct((rows, width), f32),
            jax.ShapeDtypeStruct((rows, width), f32),
            jax.ShapeDtypeStruct((parts, batch, 3, width // batch, hidden_cols), bf16),
        ],
        scratch_shapes=[
            pltpu.VMEM((width, rows), bf16),
            pltpu.VMEM((width, rows), bf16),
            pltpu.VMEM((3, width, tile), f32),
        ],
        compiler_params=pltpu.CompilerParams(vmem_limit_bytes=60 << 20),
        cost_estimate=pl.CostEstimate(
            flops=18 * rows * width * hidden_cols * parts,
            bytes_accessed=18 * rows * width + 12 * parts * width * hidden_cols,
            transcendentals=0,
        ),
        name="feed_forward",
    )(normed, cot, weights, weights, weights)


BACK_TILE = 512


def norm_again(values):
    row_mean = jnp.mean(values, -1, keepdims=True)
    centred = values - row_mean
    inverse = lax.rsqrt(jnp.mean(centred * centred, -1, keepdims=True) + EPS)
    return (centred * inverse, inverse)


def row_sum(values):
    return jnp.sum(values, 0, keepdims=True)


def place_halves(core, write, own, other):
    for index in range(2):

        @pl.when(core == index)
        def _(index=index):
            write(index, own)
            write(1 - index, other)


def mixer_back_kernel(
    core_ref, second_ref, mlp_ref, middle_ref, cot_ref, gated_ref, queries_ref, own_ref, got_ref,
    normed_ref, out_weight_ref, gain_ref,
    out_ref, low_ref, grad_ref, d_q_ref, d_own_ref, d_send_ref, wide_ref, sums_ref,
    sum_q, sum_out,
):
    step = pl.program_id(0)
    half = own_ref.shape[1]
    width = 2 * half

    @pl.when(step == 0)
    def _():
        sum_q[...] = jnp.zeros_like(sum_q)
        sum_out[...] = jnp.zeros_like(sum_out)
        sums_ref[...] = jnp.zeros_like(sums_ref)

    middle = middle_ref[...]
    out = middle + mlp_ref[...]
    out_ref[...] = out
    low_ref[...] = out.astype(bf16)
    hat, inverse = norm_again(middle)
    d_second = second_ref[...]
    grad = cot_ref[...].astype(f32) + norm_back(d_second, hat, inverse, gain_ref[...])
    grad_ref[...] = grad
    d_mix = grad.astype(bf16)
    d_gated = dot_nt(d_mix, out_weight_ref[...])
    mixed = jnp.concatenate([own_ref[...], got_ref[...]], 1).astype(f32)
    d_q = (d_gated * mixed).astype(bf16)
    d_q_ref[...] = d_q
    d_mixed = (d_gated * queries_ref[...]).astype(bf16)
    d_own_ref[...] = d_mixed[:, :half]
    d_send_ref[...] = d_mixed[:, half:]
    sum_q[...] += jnp.dot(normed_ref[...].T, d_q, preferred_element_type=f32)
    sum_out[...] += jnp.dot(gated_ref[...].T, d_mix, preferred_element_type=f32)
    sums_ref[0:1] += row_sum(d_second * hat)
    sums_ref[1:2] += row_sum(d_second)
    sums_ref[2:3] += row_sum(d_mix.astype(f32))
    sums_ref[3:4] += row_sum(d_q.astype(f32))

    @pl.when(step == pl.num_programs(0) - 1)
    def _():
        core = core_ref[0]

        def write_q(index, value):
            wide_ref[:, index * half : (index + 1) * half] = value.astype(bf16)

        def write_out(index, value):
            wide_ref[index * half : (index + 1) * half, width:] = value.astype(bf16)

        place_halves(core, write_q, sum_q[:, :half], sum_q[:, half:])
        place_halves(core, write_out, sum_out[:half], sum_out[half:])


def mixer_back(
    core, second, mlp, middle, cot, gated, queries, own, got, normed, out_weight, gain
):
    rows, width = middle.shape
    half = width // 2
    tile = min(BACK_TILE, rows)

    def rows_of(columns):
        return pl.BlockSpec((tile, columns), lambda n, core: (n, 0))

    def whole(shape):
        return pl.BlockSpec(shape, lambda n, core: (0, 0))

    wide, narrow = (rows_of(width), rows_of(half))
    return pl.pallas_call(
        mixer_back_kernel,
        grid_spec=pltpu.PrefetchScalarGridSpec(
            num_scalar_prefetch=1,
            grid=(rows // tile,),
            in_specs=[wide] * 6 + [narrow, narrow, wide, whole((width, width)), whole((1, width))],
            out_specs=[wide] * 4 + [narrow, narrow, whole((width, 2 * width)), whole((8, width))],
            scratch_shapes=[
                pltpu.VMEM((width, width), f32),
                pltpu.VMEM((width, width), f32),
            ],
        ),
        out_shape=[
            jax.ShapeDtypeStruct((rows, width), f32),
            jax.ShapeDtypeStruct((rows, width), bf16),
            jax.ShapeDtypeStruct((rows, width), f32),
            jax.ShapeDtypeStruct((rows, width), bf16),
            jax.ShapeDtypeStruct((rows, half), bf16),
            jax.ShapeDtypeStruct((rows, half), bf16),
            jax.ShapeDtypeStruct((width, 2 * width), bf16),
            jax.ShapeDtypeStruct((8, width), f32),
        ],
        compiler_params=pltpu.CompilerParams(vmem_limit_bytes=56 << 20),
        cost_estimate=pl.CostEstimate(
            flops=6 * rows * width * width, bytes_accessed=40 * rows * width, transcendentals=0
        ),
        name="mixer_back",
    )(core, second, mlp, middle, cot, gated, queries, own, got, normed, out_weight, gain)


def entry_back_kernel(
    core_ref, d_q_ref, own_ref, got_ref, normed_ref, rows_ref, grad_ref,
    q_ref, k_ref, v_ref, gain_ref,
    out_ref, low_ref, pair_ref, sums_ref,
    total,
):
    step = pl.program_id(0)
    half = own_ref.shape[2]
    width = 2 * half

    @pl.when(step == 0)
    def _():
        total[...] = jnp.zeros_like(total)
        sums_ref[...] = jnp.zeros_like(sums_ref)

    kern = jnp.concatenate([own_ref[0], got_ref[0]], 1)
    val = jnp.concatenate([own_ref[1], got_ref[1]], 1)
    d_first = (
        dot_nt(d_q_ref[...], q_ref[...]) + dot_nt(kern, k_ref[...]) + dot_nt(val, v_ref[...])
    )
    hat, inverse = norm_again(rows_ref[...].astype(f32))
    grad = grad_ref[...] + norm_back(d_first, hat, inverse, gain_ref[...])
    out_ref[...] = grad
    low_ref[...] = grad.astype(bf16)
    turned = normed_ref[...].T
    total[:, :width] += jnp.dot(turned, kern, preferred_element_type=f32)
    total[:, width:] += jnp.dot(turned, val, preferred_element_type=f32)
    sums_ref[0:1] += row_sum(d_first * hat)
    sums_ref[1:2] += row_sum(d_first)
    sums_ref[2:3] += row_sum(kern.astype(f32))
    sums_ref[3:4] += row_sum(val.astype(f32))

    @pl.when(step == pl.num_programs(0) - 1)
    def _():
        for base in (0, width):

            def write(index, value, base=base):
                pair_ref[:, base + index * half : base + (index + 1) * half] = value.astype(bf16)

            place_halves(
                core_ref[0],
                write,
                total[:, base : base + half],
                total[:, base + half : base + width],
            )


def entry_back(core, d_q, own, got, normed, rows_in, grad, q_weight, k_weight, v_weight, gain):
    rows, width = grad.shape
    half = width // 2
    tile = min(BACK_TILE, rows)
    wide = pl.BlockSpec((tile, width), lambda n, core: (n, 0))
    pairs = pl.BlockSpec((2, tile, half), lambda n, core: (0, n, 0))

    def whole(shape):
        return pl.BlockSpec(shape, lambda n, core: (0, 0))

    return pl.pallas_call(
        entry_back_kernel,
        grid_spec=pltpu.PrefetchScalarGridSpec(
            num_scalar_prefetch=1,
            grid=(rows // tile,),
            in_specs=[wide, pairs, pairs, wide, wide, wide]
            + [whole((width, width))] * 3
            + [whole((1, width))],
            out_specs=[wide, wide, whole((width, 2 * width)), whole((8, width))],
            scratch_shapes=[pltpu.VMEM((width, 2 * width), f32)],
        ),
        out_shape=[
            jax.ShapeDtypeStruct((rows, width), f32),
            jax.ShapeDtypeStruct((rows, width), bf16),
            jax.ShapeDtypeStruct((width, 2 * width), bf16),
            jax.ShapeDtypeStruct((8, width), f32),
        ],
        compiler_params=pltpu.CompilerParams(vmem_limit_bytes=56 << 20),
        cost_estimate=pl.CostEstimate(flops=0, bytes_accessed=rows * width, transcendentals=0),
        name="entry_back",
    )(core, d_q, own, got, normed, rows_in, grad, q_weight, k_weight, v_weight, gain)


MESH = pl.DeviceIdType.MESH


def opening_kernel(
    rows_ref, lengths_ref, kern_ref, val_ref,
    rows_out, lengths_out, kern_out, val_out,
    send_sem, recv_sem, local_sem,
):
    b = lax.axis_index("batch")
    x = lax.axis_index("tensor")
    z, y, c = (b // 4, lax.rem(b // 2, 2), lax.rem(b, 2))

    def device(z, y, c, x):
        return (z * 4 + y * 2 + c, x)

    far = [lax.rem(z + k, 4) for k in (1, 2, 3)]
    greeted = [device(z, y, c, 1 - x), device(z, 1 - y, c, x), device(z, y, 1 - c, x)]
    greeted += [device(z, y, 1 - c, 1 - x)] + [device(other, y, c, x) for other in far]
    barrier = pltpu.get_barrier_semaphore()
    for other in greeted:
        pl.semaphore_signal(barrier, inc=1, device_id=other, device_id_type=MESH)
    pl.semaphore_wait(barrier, len(greeted))

    def remote(source, target, slot, other):
        return pltpu.make_async_remote_copy(
            src_ref=source,
            dst_ref=target,
            send_sem=send_sem.at[slot],
            recv_sem=recv_sem.at[slot],
            device_id=other,
            device_id_type=MESH,
        )

    turned = c != x
    cross = device(z, y, 1 - c, 1 - x)
    swaps = [remote(rows_ref, rows_out, 0, cross), remote(lengths_ref, lengths_out, 1, cross)]
    def first_steps(source, target, slot, by_z):
        own = pltpu.make_async_copy(source, target.at[z, y, c, x], local_sem.at[slot - 2])
        own.start()
        base = 2 + (slot - 2) * 6
        if by_z:
            copies = [
                remote(source, target.at[z, y, c, x], base + n, device(far[n], y, c, x))
                for n in range(3)
            ]
        else:
            copies = [remote(source, target.at[z, y, c, x], base, device(z, y, c, 1 - x))]
        for item in copies:
            item.start()
        return [own] + copies

    kern_first = first_steps(kern_ref, kern_out, 2, False)
    val_first = first_steps(val_ref, val_out, 3, True)

    @pl.when(turned)
    def _():
        for item in swaps:
            item.start()

    def finish(copies):
        for item in copies:
            item.wait()

    finish(kern_first)
    kern_second = [remote(kern_out.at[z, y, c], kern_out.at[z, y, c], 3, device(z, 1 - y, c, x))]
    kern_second[0].start()
    finish(val_first)
    val_second = [
        remote(val_out.at[:, y, c, x], val_out.at[:, y, c, x], 11, device(z, 1 - y, c, x))
    ]
    val_second[0].start()
    finish(kern_second)
    kern_third = [
        remote(kern_out.at[z, :, c], kern_out.at[z, :, c], 4 + n, device(far[n], y, c, x))
        for n in range(3)
    ]
    for item in kern_third:
        item.start()
    finish(val_second)
    val_third = [
        remote(val_out.at[:, :, c, x], val_out.at[:, :, c, x], 12, device(z, y, c, 1 - x))
    ]
    val_third[0].start()
    finish(kern_third)
    kern_last = [remote(kern_out.at[:, :, c], kern_out.at[:, :, c], 7, device(z, y, 1 - c, x))]
    kern_last[0].start()
    finish(val_third)
    val_last = [remote(val_out.at[:, :, c], val_out.at[:, :, c], 13, device(z, y, 1 - c, x))]
    val_last[0].start()
    finish(kern_last)
    finish(val_last)

    @pl.when(turned)
    def _():
        finish(swaps)


def opening(rows, lengths, kern, val):
    anywhere = pl.BlockSpec(memory_space=pl.ANY)
    rows_out, lengths_out, kern_out, val_out = pl.pallas_call(
        opening_kernel,
        in_specs=[anywhere] * 4,
        out_specs=[anywhere] * 4,
        out_shape=[
            jax.ShapeDtypeStruct(rows.shape, rows.dtype),
            jax.ShapeDtypeStruct(lengths.shape, lengths.dtype),
            jax.ShapeDtypeStruct((4, 2, 2, 2) + kern.shape, bf16),
            jax.ShapeDtypeStruct((4, 2, 2, 2) + val.shape, bf16),
        ],
        scratch_shapes=[
            pltpu.SemaphoreType.DMA((14,)),
            pltpu.SemaphoreType.DMA((14,)),
            pltpu.SemaphoreType.DMA((2,)),
        ],
        compiler_params=pltpu.CompilerParams(collective_id=1, has_side_effects=True),
        name="opening",
    )(rows, lengths, kern, val)
    return (
        rows_out,
        lengths_out,
        kern_out.reshape(32 * kern.shape[0], kern.shape[1]),
        val_out.reshape(32 * val.shape[0], val.shape[1]),
    )


def closing_kernel(
    grad_ref, wide_ref, small_ref, pair_ref,
    grad_out, first_out, second_out,
    first_own, first_core, first_far, first_y, first_x, first_sum, first_half, first_one,
    second_own, second_core, second_y, second_far, second_x, second_sum, second_half, second_one,
    send_sem, recv_sem, local_sem,
):
    b = lax.axis_index("batch")
    x = lax.axis_index("tensor")
    z, y, c = (b // 4, lax.rem(b // 2, 2), lax.rem(b, 2))
    wide = wide_ref.shape[-1]

    def device(z, y, c, x):
        return (z * 4 + y * 2 + c, x)

    far = [lax.rem(z + k, 4) for k in (1, 2, 3)]
    greeted = [device(z, y, c, 1 - x), device(z, 1 - y, c, x), device(z, y, 1 - c, x)]
    greeted += [device(z, y, 1 - c, 1 - x)] + [device(other, y, c, x) for other in far]
    barrier = pltpu.get_barrier_semaphore()
    for other in greeted:
        pl.semaphore_signal(barrier, inc=1, device_id=other, device_id_type=MESH)
    pl.semaphore_wait(barrier, len(greeted))

    def remote(source, target, slot, other):
        return pltpu.make_async_remote_copy(
            src_ref=source,
            dst_ref=target,
            send_sem=send_sem.at[slot],
            recv_sem=recv_sem.at[slot],
            device_id=other,
            device_id_type=MESH,
        )

    def begin(copies):
        for item in copies:
            item.start()
        return copies

    def finish(copies):
        for item in copies:
            item.wait()

    turned = c != x
    swap = remote(grad_ref, grad_out, 0, device(z, y, 1 - c, 1 - x))
    mate = device(z, y, 1 - c, x)
    beside = device(z, 1 - y, c, x)
    across = device(z, y, c, 1 - x)
    left = pl.ds(0, wide)
    right = pl.ds(wide, small_ref.shape[-1])
    second_c = begin(
        [
            remote(pair_ref.at[:, :, 1 - c], second_core, 1, mate),
            pltpu.make_async_copy(pair_ref.at[:, :, c], second_own, local_sem.at[0]),
        ]
    )
    first_c = begin(
        [
            remote(wide_ref.at[:, :, 1 - c], first_core.at[:, :, :, :, left], 2, mate),
            remote(small_ref.at[:, :, 1 - c], first_core.at[:, :, :, :, right], 3, mate),
            pltpu.make_async_copy(
                wide_ref.at[:, :, c], first_own.at[:, :, :, :, left], local_sem.at[1]
            ),
            pltpu.make_async_copy(
                small_ref.at[:, :, c], first_own.at[:, :, :, :, right], local_sem.at[2]
            ),
        ]
    )

    @pl.when(turned)
    def _():
        swap.start()

    def join(target, own, got):
        def step(index, carry):
            target[index] = (own[index].astype(f32) + got[index].astype(f32)).astype(bf16)
            return carry

        lax.fori_loop(0, 4, step, 0)

    finish(second_c)
    join(second_sum, second_own, second_core)
    second_b = begin([remote(second_sum.at[:, 1 - y], second_y, 4, beside)])
    finish(first_c)
    join(first_sum, first_own, first_core)
    first_z = begin(
        [
            remote(first_sum.at[far[n]], first_far.at[n], 5 + n, device(far[n], y, c, x))
            for n in range(3)
        ]
    )
    finish(second_b)

    def join_y(index, carry):
        second_half[index] = (
            second_sum[index, y].astype(f32) + second_y[index].astype(f32)
        ).astype(bf16)
        return carry

    lax.fori_loop(0, 4, join_y, 0)
    second_z = begin(
        [
            remote(second_half.at[far[n]], second_far.at[n], 8 + n, device(far[n], y, c, x))
            for n in range(3)
        ]
    )
    finish(first_z)
    first_half[...] = (
        first_sum[z].astype(f32)
        + first_far[0].astype(f32)
        + first_far[1].astype(f32)
        + first_far[2].astype(f32)
    ).astype(bf16)
    first_b = begin([remote(first_half.at[1 - y], first_y, 11, beside)])
    finish(second_z)
    second_one[...] = (
        second_half[z].astype(f32)
        + second_far[0].astype(f32)
        + second_far[1].astype(f32)
        + second_far[2].astype(f32)
    ).astype(bf16)
    second_a = begin([remote(second_one.at[1 - x], second_x, 12, across)])
    finish(first_b)
    first_one[...] = (first_half[y].astype(f32) + first_y[...].astype(f32)).astype(bf16)
    first_a = begin([remote(first_one.at[1 - x], first_x, 13, across)])
    finish(second_a)
    second_out[...] = second_one[x].astype(f32) + second_x[...].astype(f32)
    finish(first_a)
    first_out[...] = first_one[x].astype(f32) + first_x[...].astype(f32)

    @pl.when(turned)
    def _():
        swap.wait()


def closing(grad, wide, small, pair):
    def cube(array):
        return array.astype(bf16).reshape(4, 2, 2, 2, array.shape[0] // 32, array.shape[1])

    rows = wide.shape[0] // 32
    first = wide.shape[1] + small.shape[1]
    second = pair.shape[1]
    anywhere = pl.BlockSpec(memory_space=pl.ANY)
    inside = pl.BlockSpec(memory_space=pltpu.VMEM)

    def room(*lead):
        return pltpu.VMEM(lead, bf16)

    return pl.pallas_call(
        closing_kernel,
        in_specs=[anywhere] * 4,
        out_specs=[anywhere, inside, inside],
        out_shape=[
            jax.ShapeDtypeStruct(grad.shape, bf16),
            jax.ShapeDtypeStruct((rows, first), f32),
            jax.ShapeDtypeStruct((rows, second), f32),
        ],
        scratch_shapes=[
            room(4, 2, 2, rows, first),
            room(4, 2, 2, rows, first),
            room(3, 2, 2, rows, first),
            room(2, rows, first),
            room(rows, first),
            room(4, 2, 2, rows, first),
            room(2, 2, rows, first),
            room(2, rows, first),
            room(4, 2, 2, rows, second),
            room(4, 2, 2, rows, second),
            room(4, 2, rows, second),
            room(3, 2, rows, second),
            room(rows, second),
            room(4, 2, 2, rows, second),
            room(4, 2, rows, second),
            room(2, rows, second),
            pltpu.SemaphoreType.DMA((14,)),
            pltpu.SemaphoreType.DMA((14,)),
            pltpu.SemaphoreType.DMA((3,)),
        ],
        compiler_params=pltpu.CompilerParams(
            collective_id=2, has_side_effects=True, vmem_limit_bytes=40 << 20
        ),
        cost_estimate=pl.CostEstimate(flops=0, bytes_accessed=0, transcendentals=0),
        name="closing",
    )(grad, cube(wide), cube(small), cube(pair))


def pad_lanes(array):
    extra = -array.shape[-1] % LANES
    if extra == 0:
        return array
    return jnp.pad(array, ((0, 0),) * (array.ndim - 1) + ((0, extra),))


BOTH = ("batch", "tensor")
SPLIT = ("tensor", "batch")


class Grid:
    def __init__(self, shape):
        self.batch = shape["batch"]
        self.tensor = shape["tensor"]
        self.paired = self.tensor == 2 and self.batch % 2 == 0
        self.cubed = self.tensor == 2 and self.batch == 16
        self.b = lax.axis_index("batch")
        self.t = lax.axis_index("tensor")
        self.core = lax.rem(self.b, 2)

    def send(self, array, move):
        count = self.batch * self.tensor
        pairs = []
        for source in range(count):
            b, t = move(source // self.tensor, source % self.tensor)
            if b * self.tensor + t != source:
                pairs.append((source, b * self.tensor + t))
        return lax.ppermute(array, BOTH, pairs)

    def to_bins(self, array):
        if not self.paired:
            return array
        got = self.send(array, lambda b, t: ((b & ~1) | t, b & 1))
        return jnp.where(self.core == self.t, array, got)

    def from_bins(self, array, low):
        if not self.paired:
            return array
        got = self.send(low, lambda b, t: ((b & ~1) | t, b & 1))
        return jnp.where(self.core == self.t, array, got.astype(f32))

    def other_core(self, array):
        return self.send(array, lambda b, t: (b ^ 1, t))


def on_device(
    shape,
    activations,
    cotangent,
    buckets,
    lengths,
    first_gain,
    first_bias,
    in_weight,
    in_bias,
    short_kernel,
    short_value,
    out_weight,
    out_bias,
    second_gain,
    second_bias,
    gate_weight,
    up_weight,
    down_weight,
):
    grid = Grid(shape)
    width = activations.shape[1]
    shard_rows = in_weight.shape[0]
    block_rows, hidden_cols = gate_weight.shape
    parts = 2 if grid.paired else grid.tensor
    channels = width // parts
    turned = grid.paired

    bin_index = ((grid.b // 2) * 2 + grid.t) if grid.paired else grid.b
    part_index = grid.core if grid.paired else grid.t
    bucket_here = buckets[bin_index]

    small = jnp.concatenate(
        [
            first_gain[:, None],
            first_bias[:, None],
            out_bias[:, None],
            second_gain[:, None],
            second_bias[:, None],
            short_kernel.T,
            short_value.T,
            in_bias.reshape(shard_rows, 3),
        ],
        1,
    )
    k_shard = jnp.concatenate([in_weight[:, width : 2 * width], pad_lanes(small)], 1)
    v_shard = in_weight[:, 2 * width :]
    if grid.cubed:
        rows_bf, seq_lengths, k_full, v_full = opening(activations, lengths, k_shard, v_shard)
        rows_bf = jnp.where(grid.core == grid.t, activations, rows_bf)
        seq_lengths = jnp.where(grid.core == grid.t, lengths, seq_lengths)
    else:
        rows_bf = grid.to_bins(activations)
        seq_lengths = grid.to_bins(lengths)
        k_full = lax.all_gather(k_shard, BOTH, axis=0, tiled=True)
        v_full = lax.all_gather(v_shard, BOTH, axis=0, tiled=True)
    seq_lengths = seq_lengths[0]
    late_rows = jnp.concatenate([in_weight[:, :width], out_weight], 0).reshape(block_rows, -1)
    late = lax.all_gather(
        jnp.concatenate([gate_weight, up_weight, down_weight.T, late_rows], 1),
        SPLIT,
        axis=0,
        tiled=True,
    ).reshape(grid.tensor, grid.batch * block_rows, -1)

    def own_first(array, axis):
        if not turned:
            return array
        return jnp.where(grid.core == 0, array, jnp.roll(array, width // 2, axis))

    def unpick(array):
        held = array.reshape(grid.tensor, grid.batch, 2, shard_rows, width)
        return [held[:, :, n].transpose(1, 0, 2, 3).reshape(width, width) for n in (0, 1)]

    rows_small = k_full[:, width : width + 14].astype(f32).T
    gain_one, bias_one, out_shift, gain_two, bias_two = (rows_small[n] for n in range(5))
    in_shift = rows_small[11:14].T.reshape(3, width)
    q_shift, k_shift, v_shift = (own_first(in_shift[n], 0) for n in range(3))
    tap_rows = own_first(rows_small[5:11], 1)
    chan_start = jnp.int32(0) if turned else grid.t * channels

    def part_of(array, axis):
        return lax.dynamic_slice_in_dim(array, chan_start, channels, axis)

    short_k = pad_lanes(part_of(tap_rows[0:3], 1))
    short_v = pad_lanes(part_of(tap_rows[3:6], 1))
    k_weight = own_first(k_full[:, :width], 1)
    v_weight = own_first(v_full, 1)

    rows_in = rows_bf.astype(f32)
    first_out, first_hat, first_inv = norm_parts(rows_in, gain_one, bias_one)
    normed_first = first_out.astype(bf16)
    rows_here = rows_in.shape[0]

    def project(weight, shift):
        return jnp.dot(normed_first, weight, preferred_element_type=f32) + shift

    if turned:
        send_weight = jnp.concatenate([k_weight[:, channels:], v_weight[:, channels:]], 1)
        send_shift = jnp.concatenate([k_shift[channels:], v_shift[channels:]])
        own_weight = jnp.concatenate([k_weight[:, :channels], v_weight[:, :channels]], 1)
        own_shift = jnp.concatenate([k_shift[:channels], v_shift[:channels]])
        kv_send = project(send_weight, send_shift).astype(bf16)
        kv_got = grid.other_core(kv_send)
        kv_own = project(own_weight, own_shift).astype(bf16)
        pieces = [kv_own, kv_got]
        place = [grid.core, 1 - grid.core]
    else:
        kv_weight = jnp.concatenate([k_weight, v_weight], 1)
        kv_shift = jnp.concatenate([k_shift, v_shift])
        kv = project(kv_weight, kv_shift).astype(bf16)
        halves = [
            pad_lanes(lax.all_to_all(item, "tensor", split_axis=1, concat_axis=0, tiled=True))
            for item in (kv[:, :width], kv[:, width:])
        ]
        pieces = [jnp.concatenate(halves, 1)]
        place = [jnp.int32(0)]
    bin_rows = pieces[0].shape[0] * len(pieces)
    tables = conv_tables(bin_rows)
    meta = jnp.concatenate([jnp.stack([bucket_here] + place), seq_lengths]).astype(jnp.int32)
    *mixed_chan, unit_spec, value_spec, norms = conv_forward(
        pieces, meta, short_k, short_v, tables
    )
    norm_part = jnp.sum(norms[:, :channels], 0) / (bin_rows // INNER) * jnp.left_shift(
        jnp.int32(1), bucket_here
    ).astype(f32)
    if turned:
        mixed_own = mixed_chan[0].reshape(rows_here, channels)
        mixed_got = grid.other_core(mixed_chan[1]).reshape(rows_here, channels)
        mixed = jnp.concatenate([mixed_own, mixed_got], 1).astype(f32)
    else:
        mixed = lax.all_to_all(
            mixed_chan[0].reshape(bin_rows, -1)[:, :channels],
            "tensor",
            split_axis=0,
            concat_axis=1,
            tiled=True,
        ).astype(f32)

    q_weight, out_full = unpick(late[:, :, 3 * hidden_cols :])
    q_weight = own_first(q_weight, 1)
    out_full = own_first(out_full, 0)
    queries = project(q_weight, q_shift)
    gated = (queries * mixed).astype(bf16)
    middle = rows_in + jnp.dot(gated, out_full, preferred_element_type=f32) + out_shift
    second_out, second_hat, second_inv = norm_parts(middle, gain_two, bias_two)
    normed_second = second_out.astype(bf16)
    cot_low = grid.to_bins(cotangent.astype(bf16))
    mlp_out, d_second, packed = feed_forward(
        normed_second, cot_low, late, hidden_cols, grid.batch
    )
    mlp_sum = lax.psum_scatter(
        packed.reshape(-1, hidden_cols), SPLIT, scatter_dimension=0, tiled=True
    ).astype(f32)

    def natural(array, axis):
        return own_first(array, axis)

    if turned:
        core = grid.core.astype(jnp.int32)[None]
        out_here, out_low, grad_middle, d_queries, d_own, d_send, wide_grad, sums = mixer_back(
            core,
            d_second,
            mlp_out,
            middle,
            cot_low,
            gated,
            queries,
            mixed_own,
            mixed_got,
            normed_first,
            out_full,
            gain_two[None],
        )
        grad_gain_two, grad_bias_two, grad_out_shift, grad_q_shift = (sums[n] for n in range(4))
        d_mixed_pieces = [d_own, grid.other_core(d_send)]
    else:
        out_here = middle + mlp_out
        second_hat, second_inv = norm_parts(middle, gain_two, bias_two)[1:]
        grad_middle = cot_low.astype(f32) + norm_back(d_second, second_hat, second_inv, gain_two)
        grad_gain_two = jnp.sum(d_second * second_hat, 0)
        grad_bias_two = jnp.sum(d_second, 0)
        d_mix = grad_middle.astype(bf16)
        d_gated = jnp.einsum("re,de->rd", d_mix, out_full, preferred_element_type=f32)
        d_mixed = (d_gated * queries).astype(bf16)
        d_mixed_pieces = [
            pad_lanes(lax.all_to_all(d_mixed, "tensor", split_axis=1, concat_axis=0, tiled=True))
        ]
        d_queries = (d_gated * mixed).astype(bf16)
        grad_out_full = jnp.einsum("rd,re->de", gated, d_mix, preferred_element_type=f32)
        grad_out_shift = jnp.sum(d_mix.astype(f32), 0)
        grad_q = jnp.einsum("rd,rk->dk", normed_first, d_queries, preferred_element_type=f32)
        grad_q_shift = jnp.sum(d_queries.astype(f32), 0)
        wide_grad = jnp.concatenate([grad_q, grad_out_full], 1)
    *d_pieces, d_taps_k, d_taps_v = conv_backward(
        d_mixed_pieces, pieces, meta, unit_spec, value_spec, norms, short_k, short_v, tables
    )
    if turned:
        grad_here, grad_low, pair_grad, sums = entry_back(
            core,
            d_queries,
            d_pieces[0],
            grid.other_core(d_pieces[1]),
            normed_first,
            rows_bf,
            grad_middle,
            q_weight,
            k_weight,
            v_weight,
            gain_one[None],
        )
        grad_gain_one, grad_bias_one, grad_k_shift, grad_v_shift = (sums[n] for n in range(4))
    else:
        d_kv = jnp.concatenate(
            [
                lax.all_to_all(
                    d_pieces[0][n][:, :channels], "tensor", split_axis=0, concat_axis=1, tiled=True
                )
                for n in (0, 1)
            ],
            1,
        )
        kv_weight = jnp.concatenate([k_weight, v_weight], 1)
        d_first = jnp.einsum(
            "rk,dk->rd", d_queries, q_weight, preferred_element_type=f32
        ) + jnp.einsum("rk,dk->rd", d_kv, kv_weight, preferred_element_type=f32)
        grad_here = grad_middle + norm_back(d_first, first_hat, first_inv, gain_one)
        grad_low = grad_here.astype(bf16)
        grad_gain_one = jnp.sum(d_first * first_hat, 0)
        grad_bias_one = jnp.sum(d_first, 0)
        pair_grad = jnp.einsum("rd,rk->dk", normed_first, d_kv, preferred_element_type=f32)
        grad_k_shift = jnp.sum(d_kv[:, :width].astype(f32), 0)
        grad_v_shift = jnp.sum(d_kv[:, width:].astype(f32), 0)
    chan_rows = jnp.concatenate(
        [d_taps_k[:, :channels], d_taps_v[:, :channels], norm_part[None]], 0
    )
    chan_full = lax.dynamic_update_slice(
        jnp.zeros((7, width), f32), chan_rows, (jnp.int32(0), chan_start)
    )
    turned_rows = jnp.concatenate(
        [chan_full, grad_q_shift[None], grad_k_shift[None], grad_v_shift[None]], 0
    )
    turned_rows = natural(turned_rows, 1)
    small_rows = jnp.concatenate(
        [
            grad_gain_one[None],
            grad_bias_one[None],
            grad_out_shift[None],
            grad_gain_two[None],
            grad_bias_two[None],
            turned_rows[:7],
            turned_rows[7:].reshape(width, 3).T,
        ],
        0,
    )
    small_grad = pad_lanes(small_rows.T)
    if turned:
        out_rows = grid.from_bins(out_here, out_low)
    else:
        out_rows = out_here
    if grid.cubed:
        swapped, first_sum, pair_sum = closing(grad_low, wide_grad, small_grad, pair_grad)
        grad_activations = jnp.where(grid.core == grid.t, grad_here, swapped.astype(f32))
        wide_sum = first_sum[:, : 2 * width]
        small_sum = first_sum[:, 2 * width :]
    else:
        grad_activations = grid.from_bins(grad_here, grad_low)
        total = lax.psum_scatter(
            jnp.concatenate([item.astype(bf16) for item in (wide_grad, small_grad, pair_grad)], 1),
            BOTH,
            scatter_dimension=0,
            tiled=True,
        ).astype(f32)
        wide_sum = total[:, : 2 * width]
        small_sum = total[:, 2 * width : 2 * width + small_grad.shape[1]]
        pair_sum = total[:, 2 * width + small_grad.shape[1] :]
    seq_count = jnp.sum(jnp.left_shift(jnp.ones_like(buckets), buckets)).astype(f32)
    return (
        out_rows,
        grad_activations,
        small_sum[:, 0],
        small_sum[:, 1],
        jnp.concatenate([wide_sum[:, :width], pair_sum], 1),
        small_sum[:, 12:15].reshape(3 * shard_rows),
        small_sum[:, 5:8].T,
        small_sum[:, 8:11].T,
        wide_sum[:, width:],
        small_sum[:, 2],
        small_sum[:, 3],
        small_sum[:, 4],
        mlp_sum[:block_rows],
        mlp_sum[block_rows : 2 * block_rows],
        mlp_sum[2 * block_rows :].T,
        small_sum[:, 11] / seq_count,
    )


def solution(mesh):
    return jax.shard_map(
        functools.partial(on_device, dict(mesh.shape)),
        mesh=mesh,
        in_specs=(
            P(("batch", "tensor"), None),
            P(("batch", "tensor"), None),
            P(),
            P("batch", None),
            P(("batch", "tensor")),
            P(("batch", "tensor")),
            P(("batch", "tensor"), None),
            P(("batch", "tensor")),
            P(None, ("batch", "tensor")),
            P(None, ("batch", "tensor")),
            P(("batch", "tensor"), None),
            P(("batch", "tensor")),
            P(("batch", "tensor")),
            P(("batch", "tensor")),
            P("batch", "tensor"),
            P("batch", "tensor"),
            P("tensor", "batch"),
        ),
        out_specs=(
            P(("batch", "tensor"), None),
            P(("batch", "tensor"), None),
            P(("batch", "tensor")),
            P(("batch", "tensor")),
            P(("batch", "tensor"), None),
            P(("batch", "tensor")),
            P(None, ("batch", "tensor")),
            P(None, ("batch", "tensor")),
            P(("batch", "tensor"), None),
            P(("batch", "tensor")),
            P(("batch", "tensor")),
            P(("batch", "tensor")),
            P("batch", "tensor"),
            P("batch", "tensor"),
            P("tensor", "batch"),
            P(("batch", "tensor")),
        ),
        check_vma=False,
    )
```
